256 devices in a mesh: row: 32 (over z, x), col: 8 (over y, core).
Axes of the slice: x: 4, y: 4, z: 8, core: 2. Of those that a mesh axis runs over, the one named last changes fastest.
Arguments:
- tokens: bfloat16 [2048, 4096], P('row', 'col'), may hold values from -6 to 6
- gate_weight: bfloat16 [4096, 14336], P('col', 'row'), may hold values from -0.09375 to 0.09375
- up_weight: bfloat16 [4096, 14336], P('col', 'row'), may hold values from -0.09375 to 0.09375
- down_weight: bfloat16 [14336, 4096], P('row', 'col'), may hold values from -0.046875 to 0.046875
- gate_mask: int32 [32, 112], replicated, may hold values 0 or 1
- up_mask: int32 [32, 112], replicated, may hold values 0 or 1
- down_mask: int32 [112, 32], replicated, may hold values 0 or 1
- out_grad: bfloat16 [2048, 4096], P('row', 'col'), may hold values from -6 to 6
Outputs:
- mixed: bfloat16 [2048, 4096], P('row', 'col')
- input_grad: bfloat16 [2048, 4096], P('row', 'col')
- gate_grad: float32 [4096, 14336], P('col', 'row')
- up_grad: float32 [4096, 14336], P('col', 'row')
- down_grad: float32 [14336, 4096], P('row', 'col')
The draws below stay inside these ranges and needn't reach their ends.
All inputs are finite; a program needn't handle non-finite values.
Results may differ from the reference program's by a relative error of at most 0.0049.
Values may be sent and summed in bfloat16 or wider, within the bound.
A program may use at most 64 MiB of HBM per device.

```python
import jax
import jax.numpy as jnp

D = 4096
FF = 14336
BLOCK = 128
TOKENS = 2048


def set_ends(entries, rng, low, high):
    longest = entries.shape.index(max(entries.shape))
    spots = []
    for shift in (0, 1):
        where = [jax.random.randint(jax.random.fold_in(rng, axis), (), 0, length) for axis, length in enumerate(entries.shape)]
        where[longest] = (where[longest] + shift) % entries.shape[longest]
        spots.append(tuple(where))
    return entries.at[spots[0]].set(low).at[spots[1]].set(high)


def shard_levels(own_key, extent, split, low, high):
    factor_of = 1.0
    for axis_at, shards_of in split:
        draws = jax.random.uniform(jax.random.fold_in(jax.random.fold_in(own_key, 6), axis_at), (shards_of,), jnp.float32, low / len(split), high / len(split))
        factor_of = factor_of * jnp.repeat(jnp.exp(draws), extent[axis_at] // shards_of).reshape((-1,) + (1,) * (len(extent) - 1 - axis_at))
    return factor_of


def centred(stream_key, dims, width, bound, pieces=(), kind=jnp.bfloat16):
    level = shard_levels(stream_key, dims, pieces, -0.22, 0.18) if pieces else 1.0
    drawn = jax.random.normal(stream_key, dims, jnp.float32) * width * level
    return jnp.minimum(jnp.maximum(drawn, -bound), bound).astype(kind)


def setup_inputs(seed: int = 0) -> dict:
    arg_keys = jax.random.split(jax.random.key(seed), 9)
    return {
        "tokens": centred(arg_keys[0], (TOKENS, D), 1.0, 6.0, ((0, 32), (1, 8))),
        "gate_weight": centred(arg_keys[1], (D, FF), D ** -0.5, 0.09375, ((0, 8), (1, 32))),
        "up_weight": centred(arg_keys[2], (D, FF), D ** -0.5, 0.09375, ((0, 8), (1, 32))),
        "down_weight": centred(arg_keys[3], (FF, D), FF ** -0.5, 0.046875, ((0, 32), (1, 8))),
        "gate_mask": set_ends((jax.random.randint(arg_keys[4], (D // BLOCK, FF // BLOCK), 0, 8) < 5).astype(jnp.int32), jax.random.fold_in(arg_keys[4], 1), 0, 1),
        "up_mask": set_ends((jax.random.randint(arg_keys[5], (D // BLOCK, FF // BLOCK), 0, 8) < 5).astype(jnp.int32), jax.random.fold_in(arg_keys[5], 1), 0, 1),
        "down_mask": set_ends((jax.random.randint(arg_keys[6], (FF // BLOCK, D // BLOCK), 0, 8) < 5).astype(jnp.int32), jax.random.fold_in(arg_keys[6], 1), 0, 1),
        "out_grad": centred(arg_keys[7], (TOKENS, D), 1.0, 6.0, ((0, 32), (1, 8))),
    }


def expand(mask):
    return jnp.repeat(jnp.repeat(mask, BLOCK, axis=0), BLOCK, axis=1)


def reference(tokens, gate_weight, up_weight, down_weight, gate_mask, up_mask, down_mask, out_grad):
    keep_gate = expand(gate_mask)
    keep_up = expand(up_mask)
    keep_down = expand(down_mask)
    zero = jnp.zeros((), jnp.bfloat16)
    kept_gate = jnp.where(keep_gate > 0, gate_weight, zero)
    kept_up = jnp.where(keep_up > 0, up_weight, zero)
    kept_down = jnp.where(keep_down > 0, down_weight, zero)
    gate = jnp.dot(tokens, kept_gate, preferred_element_type=jnp.float32)
    up = jnp.dot(tokens, kept_up, preferred_element_type=jnp.float32)
    sig = jax.nn.sigmoid(gate)
    hidden = (gate * sig * up).astype(jnp.bfloat16)
    mixed = jnp.dot(hidden, kept_down, preferred_element_type=jnp.float32).astype(jnp.bfloat16)
    hidden_grad = jnp.dot(out_grad, kept_down.T, preferred_element_type=jnp.float32)
    dgate = (hidden_grad * up * sig * (1.0 + gate * (1.0 - sig))).astype(jnp.bfloat16)
    dup = (hidden_grad * gate * sig).astype(jnp.bfloat16)
    input_grad = (jnp.dot(dgate, kept_gate.T, preferred_element_type=jnp.float32)
                  + jnp.dot(dup, kept_up.T, preferred_element_type=jnp.float32)).astype(jnp.bfloat16)
    gate_grad = keep_gate.astype(jnp.float32) * jnp.dot(tokens.T, dgate, preferred_element_type=jnp.float32)
    up_grad = keep_up.astype(jnp.float32) * jnp.dot(tokens.T, dup, preferred_element_type=jnp.float32)
    down_grad = keep_down.astype(jnp.float32) * jnp.dot(hidden.T, out_grad, preferred_element_type=jnp.float32)
    return mixed, input_grad, gate_grad, up_grad, down_grad
```

```python
import functools

import jax
import jax.numpy as jnp
from jax import lax
from jax.experimental import pallas as pl
from jax.experimental.pallas import tpu as pltpu
from jax.sharding import PartitionSpec as P

BLOCK = 128
NX, NY, NZ = 4, 4, 8
T = 32
S = NX * T
FC = 512
F = 2 * FC
U = 448
DZ = (0, 1, -1, 2, -2, 3, -3, 4)
SLOT = {d % NZ: i for i, d in enumerate(DZ)}
GROUPS = ((0,), (1, 2), (3, 4), (5, 6), (7,))
BF = jnp.bfloat16
F32 = jnp.float32
MESH = pl.DeviceIdType.MESH


def nn(a, b):
    return jnp.dot(a, b, preferred_element_type=F32)


def nt(a, b):
    return lax.dot_general(a, b, (((1,), (1,)), ((), ())), preferred_element_type=F32)


def tn(a, b):
    return lax.dot_general(a, b, (((0,), (0,)), ((), ())), preferred_element_type=F32)


def kernel(
    tok, gw, uw, dw, gm, um, dm, og,
    mixed_o, ig_o, gg_o, ug_o, dg_o,
    ta, gb, to, go, gwo, uwo, dwo, wgu, kd, mg, mu, md,
    pf, pp, pr, hd, ho, mz, mr, mr0, p2, ir, si, iz, sm, mx,
    s_ax, s_bz, s_w, s_bx, s_az, s_ry, s_ay, s_ho, s_to, s_mz, s_mzh, s_ix, s_iz, s_mx,
    r_ax, r_bz, r_w, r_bx, r_az, r_ry, r_ay, r_ho, r_to, r_mz, r_ix, r_iz, r_mx,
):
    row, col = lax.axis_index("row"), lax.axis_index("col")
    z, x = row // NX, row % NX
    y, k = col // 2, col % 2

    def dev(dz, dx, dy, core):
        r = ((z + dz + NZ) % NZ) * NX + (x + dx) % NX
        return (r, ((y + dy) % NY) * 2 + core)

    sib = dev(0, 0, 0, 1 - k)

    def send(src, dst, ss, rs, to_dev):
        pltpu.make_async_remote_copy(
            src_ref=src, dst_ref=dst, send_sem=ss, recv_sem=rs, device_id=to_dev, device_id_type=MESH
        ).start()

    def local(src, dst, sem):
        pltpu.make_async_copy(src, dst, sem).start()

    def wait(ref, sem):
        pltpu.make_async_copy(ref, ref, sem).wait()

    def rows(start, size):
        return pl.ds(pl.multiple_of(start, 32), size)

    bar = pltpu.get_barrier_semaphore()
    partners = [sib]
    partners += [dev(0, e, 0, c) for e in range(1, NX) for c in (0, 1)]
    partners += [dev(e, 0, 0, c) for e in range(1, NZ) for c in (0, 1)]
    partners += [dev(0, 0, e, k) for e in range(1, NY)]
    for p in partners:
        pl.semaphore_signal(bar, inc=1, device_id=p, device_id_type=MESH)
    pl.semaphore_wait(bar, len(partners))

    mine = rows(x * T, T)
    for e in (1, 3, 2):
        for c in (0, 1):
            send(tok.at[pl.ds(c * T, T)], ta.at[k, mine], s_ax, r_ax, dev(0, e, 0, c))
    send(tok.at[rows((1 - k) * T, T)], ta.at[k, mine], s_ax, r_ax, sib)
    local(tok.at[rows(k * T, T)], ta.at[k, mine], r_ax)
    send(og.at[rows((1 - k) * T, T)], gb.at[k, mine], s_bz, r_bz.at[0], sib)
    local(og.at[rows(k * T, T)], gb.at[k, mine], r_bz.at[0])
    for d in DZ[1:]:
        s = SLOT[-d % NZ]
        for c in (0, 1):
            send(og.at[pl.ds(c * T, T)], gb.at[k, rows(s * S + x * T, T)], s_bz, r_bz.at[s], dev(d, 0, 0, c))
    send(gw, gwo, s_w.at[0], r_w.at[0], sib)
    send(uw, uwo, s_w.at[1], r_w.at[1], sib)
    send(dw, dwo, s_w.at[2], r_w.at[2], sib)

    def forward_tokens(s):
        d = DZ[s]
        if s == 0:
            wait(ta.at[:, pl.ds(0, S)], r_ax)
            steps = [(j, e) for j in (0, 1) for e in (1, -1)]
        else:
            e = -1 if d > 0 else 1
            js = ((0, 1) if abs(d) < 3 else ((0,) if d < 0 else (1,)))
            steps = [(j, e) for j in js]
        for j in (0, 1):
            if s:
                wait(ta.at[j, pl.ds(s * S, S)], r_az.at[s, j])
            for jj, e in steps:
                if jj == j:
                    t = SLOT[(d - e) % NZ]
                    send(ta.at[j, pl.ds(s * S, S)], ta.at[j, pl.ds(t * S, S)], s_az.at[j], r_az.at[t, j], dev(e, 0, 0, k))

    def last_tokens():
        for j in (0, 1):
            wait(ta.at[j, pl.ds(7 * S, S)], r_az.at[7, j])

    def forward_grads(s):
        mine = rows(s * S + x * T, T)
        wait(gb.at[:, pl.ds(s * S, T)], r_bz.at[s])
        for e in (1, 3, 2):
            send(gb.at[:, mine], gb.at[:, mine], s_bx.at[e - 1], r_bx.at[s], dev(0, e, 0, k))

    def unit_block(shape, dim):
        return (row * U + lax.broadcasted_iota(jnp.int32, shape, dim)) // BLOCK

    def masks():
        cols = (unit_block((112, U), 1) == lax.broadcasted_iota(jnp.int32, (112, U), 0)).astype(F32)
        mg[...] = nn(gm[pl.ds(pl.multiple_of(8 * y, 8), 8), :].astype(F32), cols)
        mu[...] = nn(um[pl.ds(pl.multiple_of(8 * y, 8), 8), :].astype(F32), cols)
        left = (unit_block((U, 112), 0) == lax.broadcasted_iota(jnp.int32, (U, 112), 1)).astype(F32)
        feat = (y * F + lax.broadcasted_iota(jnp.int32, (32, F), 1)) // BLOCK
        right = (feat == lax.broadcasted_iota(jnp.int32, (32, F), 0)).astype(F32)
        md[...] = nn(nn(left, dm[...].astype(F32)), right).astype(BF)

    zero = jnp.zeros((), BF)

    def keep_weights(core, g_ref, u_ref, d_ref):
        for b in range(FC // BLOCK):
            r = pl.ds(pl.multiple_of(core * FC + b * BLOCK, BLOCK), BLOCK)
            blk = pl.ds(b * BLOCK, BLOCK)
            m = pl.ds(core * (FC // BLOCK) + b, 1)
            g = jnp.where(jnp.broadcast_to(mg[m, :], (BLOCK, U)) > 0, g_ref[blk, :].astype(F32), 0.0)
            u = jnp.where(jnp.broadcast_to(mu[m, :], (BLOCK, U)) > 0, u_ref[blk, :].astype(F32), 0.0)
            wgu[r, :] = jnp.concatenate([g, u], axis=1).astype(BF)
        c = pl.ds(pl.multiple_of(core * FC, FC), FC)
        kd[:, c] = (md[:, c].astype(F32) * d_ref[...].astype(F32)).astype(BF)

    def stage1(s):
        wait(gb.at[:, pl.ds(0, 3 * T)], r_bx.at[s])
        r = pl.ds(s * S, S)
        both = nn(ta[0, r, :], wgu[0:FC, :]) + nn(ta[1, r, :], wgu[FC:F, :])
        back = nt(gb[0, r, :], kd[:, 0:FC]) + nt(gb[1, r, :], kd[:, FC:F])
        pf[r, 0 : 2 * U] = both
        pf[r, 2 * U : 3 * U] = back
        pp[r, 0 : 2 * U] = both.astype(BF)
        pp[r, 2 * U : 3 * U] = back.astype(BF)
        for e in (1, 3, 2):
            other = (y + e) % NY
            send(pp.at[rows(s * S + other * T, T)], pr.at[e - 1, pl.ds(s * T, T)], s_ry.at[e - 1], r_ry.at[s], dev(0, 0, e, k))

    def elementwise(s):
        wait(pp.at[pl.ds(0, 3 * T)], r_ry.at[s])
        mine = rows(s * S + y * T, T)
        r = pl.ds(s * T, T)
        tot = (pf[mine, :] + pr[0, r, :].astype(F32)) + (pr[1, r, :].astype(F32) + pr[2, r, :].astype(F32))
        gate, up, hg = tot[:, 0:U], tot[:, U : 2 * U], tot[:, 2 * U : 3 * U]
        sig = 1.0 / (1.0 + jnp.exp(-gate))
        act = gate * sig
        dgate = hg * up * sig * (1.0 + gate * (1.0 - sig))
        dup = hg * act
        hd[mine, :] = jnp.concatenate([dgate, dup, act * up], axis=1).astype(BF)

    def share(s):
        mine = rows(s * S + y * T, T)
        for e in (1, 3, 2):
            send(hd.at[mine], hd.at[mine], s_ay.at[e - 1], r_ay.at[s], dev(0, 0, e, k))

    def stage2(s):
        d = DZ[s]
        r = pl.ds(s * S, S)
        wait(hd.at[pl.ds(0, 3 * T)], r_ay.at[s])
        send(hd.at[r], ho.at[r], s_ho, r_ho, sib)
        part = nn(hd[r, 2 * U : 3 * U], kd[...])
        if s == 7:
            mz[r, :] = part.astype(BF)
            send(mz.at[r, 0:FC], mr.at[pl.ds(6 * S, S), 0:FC], s_mzh.at[0], r_mz.at[6], dev(-1, 0, 0, k))
            send(mz.at[r, FC:F], mr.at[pl.ds(5 * S, S), FC:F], s_mzh.at[1], r_mz.at[5], dev(1, 0, 0, k))
        elif abs(d) == 3:
            half = slice(0, FC) if d < 0 else slice(FC, F)
            rest = slice(FC, F) if d < 0 else slice(0, FC)
            mz[r, rest] = part[:, rest].astype(BF)
            wait(mr.at[r, half], r_mz.at[s])
            mz[r, half] = (part[:, half] + mr[r, half].astype(F32)).astype(BF)
            t = 4 if d < 0 else 3
            send(mz.at[r], mr.at[pl.ds(t * S, S)], s_mz.at[0 if d < 0 else 1], r_mz.at[t], dev(-1 if d < 0 else 1, 0, 0, k))
        elif s:
            wait(mr.at[r], r_mz.at[s])
            mz[r, :] = (part + mr[r, :].astype(F32)).astype(BF)
            down = d < 0
            if abs(d) == 2:
                t = 2 if down else 1
                send(mz.at[r], mr.at[pl.ds(t * S, S)], s_mz.at[0 if down else 1], r_mz.at[t], dev(-1 if down else 1, 0, 0, k))
            else:
                send(mz.at[r], mr0.at[0 if down else 1], s_mz.at[0 if down else 1], r_mz.at[0 if down else 7], dev(-1 if down else 1, 0, 0, k))
        else:
            wait(mr0.at[0], r_mz.at[0])
            wait(mr0.at[1], r_mz.at[7])
            sm[...] = part + (mr0[0].astype(F32) + mr0[1].astype(F32))
            for e in (1, 3, 2):
                other = (x + e) % NX
                for c in (0, 1):
                    send(sm.at[rows(other * T, T), c * FC : (c + 1) * FC], mx.at[k, mine], s_mx, r_mx, dev(0, e, 0, c))
            for c in (0, 1):

                @pl.when(k == c)
                def _():
                    send(sm.at[mine, (1 - c) * FC : (2 - c) * FC], mx.at[c, mine], s_mx, r_mx, sib)
                    local(sm.at[mine, c * FC : (c + 1) * FC], mx.at[c, mine], r_mx)

    def stage2_inputs(s):
        r = pl.ds(s * S, S)
        p2[r, :] = nt(hd[r, 0 : 2 * U], wgu[...]).astype(BF)
        for e in (1, 3, 2):
            other = (x + e) % NX
            send(p2.at[rows(s * S + other * T, T)], ir.at[e - 1, pl.ds(s * T, T)], s_ix.at[e - 1], r_ix.at[s], dev(0, e, 0, k))

    def reduce_inputs(s):
        d = DZ[s]
        wait(p2.at[pl.ds(0, 3 * T)], r_ix.at[s])
        r = pl.ds(s * T, T)
        own = p2[rows(s * S + x * T, T), :].astype(F32)
        si[r, :] = ((own + ir[0, r, :].astype(F32)) + (ir[1, r, :].astype(F32) + ir[2, r, :].astype(F32))).astype(BF)
        t = SLOT[-d % NZ]
        if s:
            for c in (0, 1):
                send(si.at[r, c * FC : (c + 1) * FC], iz.at[k, pl.ds(t * T, T)], s_iz, r_iz, dev(d, 0, 0, c))
        else:
            for c in (0, 1):

                @pl.when(k == c)
                def _():
                    send(si.at[r, (1 - c) * FC : (2 - c) * FC], iz.at[c, r], s_iz, r_iz, sib)
                    local(si.at[r, c * FC : (c + 1) * FC], iz.at[c, r], r_iz)

    masks()
    keep_weights(k, gw, uw, dw)
    forward_tokens(0)
    forward_grads(0)
    for s in GROUPS[1]:
        forward_grads(s)
    wait(gwo, r_w.at[0])
    wait(uwo, r_w.at[1])
    wait(dwo, r_w.at[2])
    keep_weights(1 - k, gwo, uwo, dwo)
    stage1(0)
    for s in GROUPS[1]:
        forward_tokens(s)
    for s in GROUPS[2]:
        forward_grads(s)
    for s in GROUPS[1]:
        stage1(s)
    elementwise(0)
    for s in GROUPS[2]:
        forward_tokens(s)
    for s in GROUPS[3] + GROUPS[4]:
        forward_grads(s)
    for s in GROUPS[2]:
        stage1(s)
    for s in GROUPS[1]:
        elementwise(s)
    for s in GROUPS[3]:
        forward_tokens(s)
    for s in GROUPS[3]:
        stage1(s)
    for s in GROUPS[2]:
        elementwise(s)
    last_tokens()
    stage1(7)
    for s in GROUPS[3]:
        elementwise(s)
    elementwise(7)
    share(7)
    for s in GROUPS[3]:
        share(s)
    send(ta.at[1 - k], to, s_to.at[0], r_to.at[0], sib)
    send(gb.at[1 - k], go, s_to.at[1], r_to.at[1], sib)
    for s in GROUPS[2]:
        share(s)
    for i in (4, 3, 2, 1, 0):
        for s in GROUPS[i]:
            stage2(s)
        if i >= 2:
            for s in GROUPS[i - 2]:
                share(s) if i - 2 < 2 else None
        for s in GROUPS[i]:
            stage2_inputs(s)
        if i < 4:
            for s in GROUPS[i + 1]:
                reduce_inputs(s)
    reduce_inputs(0)

    wait(to, r_to.at[0])
    wait(go, r_to.at[1])
    wait(ho, r_ho)
    for b in range(FC // BLOCK):
        c = pl.ds(b * BLOCK, BLOCK)
        grad = tn(ta[k, :, c], hd[:, 0 : 2 * U]) + tn(to[:, c], ho[:, 0 : 2 * U])
        m = pl.ds(k * (FC // BLOCK) + b, 1)
        gg_o[c, :] = jnp.where(jnp.broadcast_to(mg[m, :], (BLOCK, U)) > 0, grad[:, 0:U], 0.0)
        ug_o[c, :] = jnp.where(jnp.broadcast_to(mu[m, :], (BLOCK, U)) > 0, grad[:, U : 2 * U], 0.0)
    grad = tn(hd[:, 2 * U : 3 * U], gb[k]) + tn(ho[:, 2 * U : 3 * U], go[...])
    dg_o[...] = grad * md[:, pl.ds(pl.multiple_of(k * FC, FC), FC)].astype(F32)

    wait(mx, r_mx)
    for c in (0, 1):
        part = [mx[c, i * T : (i + 1) * T, :] for i in range(NX)]
        mixed_o[c * T : (c + 1) * T, :] = ((part[0] + part[1]) + (part[2] + part[3])).astype(BF)
    wait(iz, r_iz)
    for c in (0, 1):
        part = [iz[c, i * T : (i + 1) * T, :].astype(F32) for i in range(NZ)]
        low = (part[0] + part[1]) + (part[2] + part[3])
        high = (part[4] + part[5]) + (part[6] + part[7])
        ig_o[c * T : (c + 1) * T, :] = (low + high).astype(BF)

    wait(ta.at[0, pl.ds(0, 7 * T)], s_ax)
    wait(gb.at[0, pl.ds(0, 15 * T)], s_bz)
    wait(gwo, s_w.at[0])
    wait(uwo, s_w.at[1])
    wait(dwo, s_w.at[2])
    for e in range(3):
        wait(gb.at[:, pl.ds(0, 8 * T)], s_bx.at[e])
        wait(pp.at[pl.ds(0, 8 * T)], s_ry.at[e])
        wait(hd.at[pl.ds(0, 8 * T)], s_ay.at[e])
        wait(p2.at[pl.ds(0, 8 * T)], s_ix.at[e])
    for j in (0, 1):
        wait(ta.at[j, pl.ds(0, 7 * S)], s_az.at[j])
        wait(to, s_to.at[j])
        wait(mz.at[pl.ds(0, 3 * S)], s_mz.at[j])
        wait(mz.at[pl.ds(0, S), 0:FC], s_mzh.at[j])
    wait(ho, s_ho)
    wait(gb.at[0, pl.ds(0, 15 * T)], s_iz)
    wait(ta.at[:, pl.ds(0, 7 * T)], s_mx)


def per_device(tokens, gate_weight, up_weight, down_weight, gate_mask, up_mask, down_mask, out_grad):
    vmem = pl.BlockSpec(memory_space=pltpu.VMEM)
    dma = pltpu.SemaphoreType.DMA
    v = pltpu.VMEM
    return pl.pallas_call(
        kernel,
        out_shape=(
            jax.ShapeDtypeStruct((2 * T, FC), BF),
            jax.ShapeDtypeStruct((2 * T, FC), BF),
            jax.ShapeDtypeStruct((FC, U), F32),
            jax.ShapeDtypeStruct((FC, U), F32),
            jax.ShapeDtypeStruct((U, FC), F32),
        ),
        in_specs=[vmem] * 8,
        out_specs=(vmem,) * 5,
        scratch_shapes=[
            v((2, NZ * S, FC), BF),
            v((2, NZ * S, FC), BF),
            v((NZ * S, FC), BF),
            v((NZ * S, FC), BF),
            v((FC, U), BF),
            v((FC, U), BF),
            v((U, FC), BF),
            v((F, 2 * U), BF),
            v((U, F), BF),
            v((8, U), F32),
            v((8, U), F32),
            v((U, F), BF),
            v((NZ * S, 3 * U), F32),
            v((NZ * S, 3 * U), BF),
            v((3, NZ * T, 3 * U), BF),
            v((NZ * S, 3 * U), BF),
            v((NZ * S, 3 * U), BF),
            v((NZ * S, F), BF),
            v((NZ * S, F), BF),
            v((2, S, F), BF),
            v((NZ * S, F), BF),
            v((3, NZ * T, F), BF),
            v((NZ * T, F), BF),
            v((2, NZ * T, FC), BF),
            v((S, F), F32),
            v((2, S, FC), F32),
            dma, dma, dma((3,)), dma((3,)), dma((2,)), dma((3,)), dma((3,)), dma, dma((2,)), dma((2,)), dma((2,)), dma((3,)), dma, dma,
            dma, dma((8,)), dma((3,)), dma((8,)), dma((8, 2)), dma((8,)), dma((8,)), dma, dma((2,)), dma((8,)), dma((8,)), dma, dma,
        ],
        compiler_params=pltpu.CompilerParams(
            collective_id=0, has_side_effects=True, vmem_limit_bytes=60 << 20
        ),
        cost_estimate=pl.CostEstimate(flops=9_000_000_000, bytes_accessed=8 << 20, transcendentals=120_000),
        name="sublayer",
    )(tokens, gate_weight, up_weight, down_weight, gate_mask, up_mask, down_mask, out_grad)


def solution(mesh):
    return jax.shard_map(
        per_device,
        mesh=mesh,
        in_specs=(
            P("row", "col"), P("col", "row"), P("col", "row"), P("row", "col"), P(), P(), P(), P("row", "col"),
        ),
        out_specs=(P("row", "col"), P("row", "col"), P("col", "row"), P("col", "row"), P("row", "col")),
        check_vma=False,
    )
```

```python
import functools

import jax
import jax.numpy as jnp
from jax import lax
from jax.experimental import pallas as pl
from jax.experimental.pallas import tpu as pltpu
from jax.sharding import PartitionSpec as P

BLOCK = 128
NX, NY, NZ = 4, 4, 8
H = 32
NC = 2
T = H // NC
S = NX * T
NS = NC * NZ
FC = 512
F = 2 * FC
U = 448
UP = 512
W = 2 * U + UP
DZ = (0, 1, -1, 2, -2, 3, -3, 4)
SLOT = {d % NZ: i for i, d in enumerate(DZ)}
GROUPS = ((0,), (1, 2), (3, 4), (5, 6), (7,))
ORDER = (
    "A0 G0 A1 W",
    "B00 G1 M B01",
    "F00 N B02 P00",
    "F01 B03 P01 F02",
    "P02 B04 F10 B10",
    "F03 P03 B11 F04",
    "P04 E02 E01 B12",
    "F11 S02 E04 S04",
    "E03 F12 S03 B13",
    "E00 P12 F13 Q04",
    "Q03 S01 B14 P11",
    "Q02 Z04 F14 P14",
    "Z03 P13 I03 E12",
    "I04 E14 S14 S00",
    "Z02 I02 E13 S13",
    "Q01 E11 Z01 Q14",
    "I01 S12 I14 P10",
    "Q00 Z14 I00 Q13",
    "Z13 I13 R02 S11",
    "Z00 Q12 Z12 E10",
    "R01 I12 S10 X",
    "R04 Q11 I11 Z11",
    "Q10 R14 R13 I10",
    "R00 Z10 R03 R12",
    "R10 R11",
)
BF = jnp.bfloat16
F32 = jnp.float32
MESH = pl.DeviceIdType.MESH


def nn(a, b):
    return jnp.dot(a, b, preferred_element_type=F32)


def nt(a, b):
    return lax.dot_general(a, b, (((1,), (1,)), ((), ())), preferred_element_type=F32)


def tn(a, b):
    return lax.dot_general(a, b, (((0,), (0,)), ((), ())), preferred_element_type=F32)


def kernel(
    tok, gw, uw, dw, gm, um, dm, og,
    mixed_o, ig_o, gg_o, ug_o, dg_o,
    ta, gb, to, go, gwo, uwo, dwo, wgu, kd, keep,
    pf, pp, pr, hd, ho, mp, mz, mr, mr0, p2, ir, si, iz, sm, mx,
    s_ax, s_bz, s_w, s_bx, s_bh, s_az, s_ry, s_ay, s_ho, s_to, s_mz, s_mzh, s_ix, s_iz, s_mx,
    r_ax, r_bz, r_w, r_bx, r_az, r_ry, r_ay, r_ho, r_to, r_mz, r_ix, r_iz, r_mx,
):
    row, col = lax.axis_index("row"), lax.axis_index("col")
    z, x = row // NX, row % NX
    y, k = col // 2, col % 2

    def dev(dz, dx, dy, core):
        r = ((z + dz + NZ) % NZ) * NX + (x + dx) % NX
        return (r, ((y + dy) % NY) * 2 + core)

    sib = dev(0, 0, 0, 1 - k)

    def send(src, dst, ss, rs, to_dev):
        pltpu.make_async_remote_copy(
            src_ref=src, dst_ref=dst, send_sem=ss, recv_sem=rs, device_id=to_dev, device_id_type=MESH
        ).start()

    def local(src, dst, sem):
        pltpu.make_async_copy(src, dst, sem).start()

    def wait(ref, sem):
        pltpu.make_async_copy(ref, ref, sem).wait()

    def rows(start, size):
        return pl.ds(pl.multiple_of(start, 16), size)

    bar = pltpu.get_barrier_semaphore()
    partners = [sib]
    partners += [dev(0, e, 0, c) for e in range(1, NX) for c in (0, 1)]
    partners += [dev(e, 0, 0, c) for e in range(1, NZ) for c in (0, 1)]
    partners += [dev(0, 0, e, k) for e in range(1, NY)]
    for p in partners:
        pl.semaphore_signal(bar, inc=1, device_id=p, device_id_type=MESH)
    pl.semaphore_wait(bar, len(partners))

    def part_of(core, c):
        return rows(core * H + c * T, T)

    def block(c, s):
        return rows((c * NZ + s) * S + x * T, T)

    def start_tokens(c):
        mine = block(c, 0)
        for e in (1, 3, 2):
            for core in (0, 1):
                send(tok.at[part_of(core, c)], ta.at[k, mine], s_ax, r_ax.at[c], dev(0, e, 0, core))
        send(tok.at[part_of(1 - k, c)], ta.at[k, mine], s_ax, r_ax.at[c], sib)
        local(tok.at[part_of(k, c)], ta.at[k, mine], r_ax.at[c])

    def start_grads(c):
        send(og.at[part_of(1 - k, c)], gb.at[k, block(c, 0)], s_bz, r_bz.at[c, 0], sib)
        local(og.at[part_of(k, c)], gb.at[k, block(c, 0)], r_bz.at[c, 0])
        for e in (1, -1):
            t = SLOT[-e % NZ]
            for core in (0, 1):
                send(og.at[part_of(core, c)], gb.at[k, block(c, t)], s_bz, r_bz.at[c, t], dev(e, 0, 0, core))

    def forward_tokens(c, s):
        d = DZ[s]
        r = pl.ds((c * NZ + s) * S, S)
        if s == 0:
            wait(ta.at[:, r], r_ax.at[c])
        for j in (0, 1):
            if s:
                wait(ta.at[j, r], r_az.at[c, s, j])
            ahead = (1, -1) if s == 0 else (-1 if d > 0 else 1,)
            if s == 7 or (abs(d) == 3 and (d < 0) != (j == 1)):
                ahead = ()
            for e in ahead:
                t = SLOT[(d - e) % NZ]
                send(ta.at[j, r], ta.at[j, pl.ds((c * NZ + t) * S, S)], s_az.at[j], r_az.at[c, t, j], dev(e, 0, 0, k))

    def forward_grads(c, s):
        d = DZ[s]
        mine = block(c, s)
        wait(gb.at[:, pl.ds(0, T)], r_bz.at[c, s])
        e = -1 if d > 0 else 1
        if 0 < abs(d) < 4:
            t = SLOT[(d - e) % NZ]
            there = block(c, t)
            if abs(d) < 3:
                send(gb.at[:, mine], gb.at[:, there], s_bh.at[0], r_bz.at[c, t], dev(e, 0, 0, k))
            else:
                j = 0 if d < 0 else 1
                send(gb.at[j, mine], gb.at[j, there], s_bh.at[1], r_bz.at[c, t], dev(e, 0, 0, k))
        for e in (1, 3, 2):
            send(gb.at[:, mine], gb.at[:, mine], s_bx.at[e - 1], r_bx.at[c, s], dev(0, e, 0, k))

    def start_weights():
        send(gw, gwo, s_w.at[0], r_w.at[0], sib)
        send(uw, uwo, s_w.at[1], r_w.at[1], sib)
        send(dw, dwo, s_w.at[2], r_w.at[2], sib)

    def masks():
        unit = (row * U + lax.broadcasted_iota(jnp.int32, (U, 112), 0)) // BLOCK
        left = (unit == lax.broadcasted_iota(jnp.int32, (U, 112), 1)).astype(F32)
        feat = (y * F + lax.broadcasted_iota(jnp.int32, (32, F), 1)) // BLOCK
        right = (feat == lax.broadcasted_iota(jnp.int32, (32, F), 0)).astype(F32)
        for i, ref in enumerate((gm, um, dm)):
            keep[i] = nn(nt(left, ref[...].astype(F32)), right).astype(BF)

    def keep_weights(core, g_ref, u_ref, d_ref):
        c = pl.ds(pl.multiple_of(core * FC, FC), FC)
        wgu[0:U, c] = keep[0, :, c] * g_ref[...]
        wgu[U : 2 * U, c] = keep[1, :, c] * u_ref[...]
        kd[0:U, c] = keep[2, :, c] * d_ref[...]
        kd[U:UP, c] = jnp.zeros((UP - U, FC), BF)

    def stage1(c, slots):
        r = pl.ds((c * NZ + slots[0]) * S, len(slots) * S)
        for s in slots:
            wait(gb.at[:, pl.ds(0, 3 * T)], r_bx.at[c, s])
        both = nt(ta[0, r, :], wgu[:, 0:FC]) + nt(ta[1, r, :], wgu[:, FC:F])
        back = nt(gb[0, r, :], kd[:, 0:FC]) + nt(gb[1, r, :], kd[:, FC:F])
        pf[r, 0 : 2 * U] = both
        pf[r, 2 * U : W] = back
        pp[r, 0 : 2 * U] = both.astype(BF)
        pp[r, 2 * U : W] = back.astype(BF)
        for s in slots:
            g = c * NZ + s
            for e in (1, 3, 2):
                other = (y + e) % NY
                send(pp.at[rows(g * S + other * T, T)], pr.at[e - 1, pl.ds(g * T, T)], s_ry.at[e - 1], r_ry.at[c, s], dev(0, 0, e, k))

    def elementwise(c, s):
        g = c * NZ + s
        wait(pp.at[pl.ds(0, 3 * T)], r_ry.at[c, s])
        mine = rows(g * S + y * T, T)
        r = pl.ds(g * T, T)
        tot = (pf[mine, :] + pr[0, r, :].astype(F32)) + (pr[1, r, :].astype(F32) + pr[2, r, :].astype(F32))
        gate, up, hg = tot[:, 0:U], tot[:, U : 2 * U], tot[:, 2 * U : 3 * U]
        sig = 1.0 / (1.0 + jnp.exp(-gate))
        act = gate * sig
        dgate = hg * up * sig * (1.0 + gate * (1.0 - sig))
        dup = hg * act
        hd[mine, :] = jnp.concatenate([dgate, dup, act * up, jnp.zeros((T, UP - U), F32)], axis=1).astype(BF)

    def share(c, s):
        g = c * NZ + s
        mine = rows(g * S + y * T, T)
        for e in (1, 3, 2):
            send(hd.at[mine], hd.at[mine], s_ay.at[e - 1], r_ay.at[c, s], dev(0, 0, e, k))

    def stage2(c, slots):
        r = pl.ds((c * NZ + slots[0]) * S, len(slots) * S)
        for s in slots:
            wait(hd.at[pl.ds(0, 3 * T)], r_ay.at[c, s])
        mp[r, :] = nn(hd[r, 2 * U : W], kd[...])
        p2[r, :] = nn(hd[r, 0 : 2 * U], wgu[...]).astype(BF)
        send(hd.at[r], ho.at[r], s_ho, r_ho, sib)

    def send_inputs(c, s):
        g = c * NZ + s
        for e in (1, 3, 2):
            other = (x + e) % NX
            send(p2.at[rows(g * S + other * T, T)], ir.at[e - 1, pl.ds(g * T, T)], s_ix.at[e - 1], r_ix.at[c, s], dev(0, e, 0, k))

    def pass_mixed(c, s):
        d = DZ[s]
        r = pl.ds((c * NZ + s) * S, S)
        way = 0 if d < 0 else 1
        ahead = dev(-1 if d < 0 else 1, 0, 0, k)
        if s == 7:
            mz[r, :] = mp[r, :].astype(BF)
            for way, t in ((0, 6), (1, 5)):
                half = slice(way * FC, (way + 1) * FC)
                there = pl.ds((c * NZ + t) * S, S)
                send(mz.at[r, half], mr.at[there, half], s_mzh.at[way], r_mz.at[c, t], dev(2 * way - 1, 0, 0, k))
        elif s:
            if abs(d) == 3:
                half = slice(way * FC, (way + 1) * FC)
                rest = slice((1 - way) * FC, (2 - way) * FC)
                mz[r, rest] = mp[r, rest].astype(BF)
                wait(mr.at[r, half], r_mz.at[c, s])
                mz[r, half] = (mp[r, half] + mr[r, half].astype(F32)).astype(BF)
            else:
                wait(mr.at[r], r_mz.at[c, s])
                mz[r, :] = (mp[r, :] + mr[r, :].astype(F32)).astype(BF)
            if abs(d) == 1:
                send(mz.at[r], mr0.at[c, way], s_mz.at[way], r_mz.at[c, 7 * way], ahead)
            else:
                t = s - 2
                send(mz.at[r], mr.at[pl.ds((c * NZ + t) * S, S)], s_mz.at[way], r_mz.at[c, t], ahead)
        else:
            wait(mr0.at[c, 0], r_mz.at[c, 0])
            wait(mr0.at[c, 1], r_mz.at[c, 7])
            tot = mp[r, :] + (mr0[c, 0].astype(F32) + mr0[c, 1].astype(F32))
            sm[c, 0] = tot[:, 0:FC]
            sm[c, 1] = tot[:, FC:F]
            mine = rows(x * T, T)
            for e in (1, 3, 2):
                other = rows((x + e) % NX * T, T)
                for core in (0, 1):
                    send(sm.at[c, core, other], mx.at[c, k, mine], s_mx, r_mx.at[c], dev(0, e, 0, core))
            send(sm.at[c, 1 - k, mine], mx.at[c, k, mine], s_mx, r_mx.at[c], sib)
            local(sm.at[c, k, mine], mx.at[c, k, mine], r_mx.at[c])

    def reduce_inputs(c, s):
        d = DZ[s]
        g = c * NZ + s
        wait(p2.at[pl.ds(0, 3 * T)], r_ix.at[c, s])
        r = pl.ds(g * T, T)
        own = p2[rows(g * S + x * T, T), :].astype(F32)
        tot = ((own + ir[0, r, :].astype(F32)) + (ir[1, r, :].astype(F32) + ir[2, r, :].astype(F32))).astype(BF)
        si[0, r, :] = tot[:, 0:FC]
        si[1, r, :] = tot[:, FC:F]
        t = pl.ds((c * NZ + SLOT[-d % NZ]) * T, T)
        if s:
            for core in (0, 1):
                send(si.at[core, r], iz.at[k, t], s_iz, r_iz.at[c], dev(d, 0, 0, core))
        else:
            send(si.at[1 - k, r], iz.at[k, t], s_iz, r_iz.at[c], sib)
            local(si.at[k, r], iz.at[k, t], r_iz.at[c])

    def each(step, c, g):
        for s in GROUPS[g]:
            step(c, s)

    def finish_weights():
        wait(gwo, r_w.at[0])
        wait(uwo, r_w.at[1])
        wait(dwo, r_w.at[2])
        keep_weights(1 - k, gwo, uwo, dwo)

    def swap_inputs():
        send(ta.at[1 - k], to, s_to.at[0], r_to.at[0], sib)
        send(gb.at[1 - k], go, s_to.at[1], r_to.at[1], sib)

    def begin():
        masks()
        keep_weights(k, gw, uw, dw)

    steps = {
        "A": start_tokens,
        "G": start_grads,
        "F": lambda c, g: each(forward_tokens, c, g),
        "B": lambda c, g: each(forward_grads, c, g),
        "P": lambda c, g: stage1(c, GROUPS[g]),
        "E": lambda c, g: each(elementwise, c, g),
        "S": lambda c, g: each(share, c, g),
        "Q": lambda c, g: stage2(c, GROUPS[g]),
        "I": lambda c, g: each(send_inputs, c, g),
        "Z": lambda c, g: each(pass_mixed, c, g),
        "R": lambda c, g: each(reduce_inputs, c, g),
        "W": start_weights,
        "M": begin,
        "N": finish_weights,
        "X": swap_inputs,
    }
    for line in ORDER:
        for step in line.split():
            steps[step[0]](*map(int, step[1:]))

    wait(to, r_to.at[0])
    wait(go, r_to.at[1])
    wait(ho, r_ho)
    own = pl.ds(pl.multiple_of(k * FC, FC), FC)
    for i, out in enumerate((gg_o, ug_o)):
        c = slice(i * U, (i + 1) * U)
        out[...] = (tn(hd[:, c], ta[k]) + tn(ho[:, c], to[...])) * keep[i, :, own].astype(F32)
    c = slice(2 * U, 3 * U)
    dg_o[...] = (tn(hd[:, c], gb[k]) + tn(ho[:, c], go[...])) * keep[2, :, own].astype(F32)

    for c in range(NC):
        wait(mx.at[c], r_mx.at[c])
        for core in (0, 1):
            part = [mx[c, core, i * T : (i + 1) * T, :] for i in range(NX)]
            there = slice(core * H + c * T, core * H + (c + 1) * T)
            mixed_o[there, :] = ((part[0] + part[1]) + (part[2] + part[3])).astype(BF)
    for c in range(NC):
        wait(iz.at[:, pl.ds(c * NZ * T, NZ * T)], r_iz.at[c])
        for core in (0, 1):
            part = [iz[core, (c * NZ + i) * T : (c * NZ + i + 1) * T, :].astype(F32) for i in range(NZ)]
            low = (part[0] + part[1]) + (part[2] + part[3])
            high = (part[4] + part[5]) + (part[6] + part[7])
            there = slice(core * H + c * T, core * H + (c + 1) * T)
            ig_o[there, :] = (low + high).astype(BF)

    wait(ta.at[0, pl.ds(0, 7 * NC * T)], s_ax)
    wait(ta.at[0, pl.ds(0, 5 * NC * T)], s_bz)
    wait(gb.at[:, pl.ds(0, 4 * NC * T)], s_bh.at[0])
    wait(gb.at[0, pl.ds(0, 2 * NC * T)], s_bh.at[1])
    for i in range(3):
        wait((gwo, uwo, dwo)[i], s_w.at[i])
        wait(gb.at[:, pl.ds(0, NS * T)], s_bx.at[i])
        wait(pp.at[pl.ds(0, NS * T)], s_ry.at[i])
        wait(hd.at[pl.ds(0, NS * T)], s_ay.at[i])
        wait(p2.at[pl.ds(0, NS * T)], s_ix.at[i])
    for j in (0, 1):
        wait(ta.at[j, pl.ds(0, 7 * NC * S)], s_az.at[j])
        wait(to, s_to.at[j])
        wait(mz.at[pl.ds(0, 3 * NC * S)], s_mz.at[j])
        wait(mz.at[pl.ds(0, NC * S), 0:FC], s_mzh.at[j])
    wait(ho, s_ho)
    wait(gb.at[0, pl.ds(0, 15 * NC * T)], s_iz)
    wait(ta.at[:, pl.ds(0, 7 * NC * T)], s_mx)


def per_device(tokens, gate_weight, up_weight, down_weight, gate_mask, up_mask, down_mask, out_grad):
    vmem = pl.BlockSpec(memory_space=pltpu.VMEM)
    dma = pltpu.SemaphoreType.DMA
    v = pltpu.VMEM
    mixed, input_grad, gate_grad, up_grad, down_grad = pl.pallas_call(
        kernel,
        out_shape=(
            jax.ShapeDtypeStruct((2 * H, FC), BF),
            jax.ShapeDtypeStruct((2 * H, FC), BF),
            jax.ShapeDtypeStruct((U, FC), F32),
            jax.ShapeDtypeStruct((U, FC), F32),
            jax.ShapeDtypeStruct((U, FC), F32),
        ),
        in_specs=[vmem] * 8,
        out_specs=(vmem,) * 5,
        scratch_shapes=[
            v((2, NS * S, FC), BF),
            v((2, NS * S, FC), BF),
            v((NS * S, FC), BF),
            v((NS * S, FC), BF),
            v((U, FC), BF),
            v((U, FC), BF),
            v((U, FC), BF),
            v((2 * U, F), BF),
            v((UP, F), BF),
            v((3, U, F), BF),
            v((NS * S, W), F32),
            v((NS * S, W), BF),
            v((3, NS * T, W), BF),
            v((NS * S, W), BF),
            v((NS * S, W), BF),
            v((NS * S, F), F32),
            v((NS * S, F), BF),
            v((NS * S, F), BF),
            v((NC, 2, S, F), BF),
            v((NS * S, F), BF),
            v((3, NS * T, F), BF),
            v((2, NS * T, FC), BF),
            v((2, NS * T, FC), BF),
            v((NC, 2, S, FC), F32),
            v((NC, 2, S, FC), F32),
            dma, dma, dma((3,)), dma((3,)), dma((2,)), dma((2,)), dma((3,)), dma((3,)), dma, dma((2,)), dma((2,)), dma((2,)), dma((3,)), dma, dma,
            dma((NC,)), dma((NC, 8)), dma((3,)), dma((NC, 8)), dma((NC, 8, 2)), dma((NC, 8)), dma((NC, 8)), dma, dma((2,)), dma((NC, 8)), dma((NC, 8)), dma((NC,)), dma((NC,)),
        ],
        compiler_params=pltpu.CompilerParams(
            collective_id=0, has_side_effects=True, vmem_limit_bytes=60 << 20
        ),
        cost_estimate=pl.CostEstimate(flops=9_000_000_000, bytes_accessed=8 << 20, transcendentals=120_000),
        name="sublayer",
    )(tokens, gate_weight.T, up_weight.T, down_weight, gate_mask, up_mask, down_mask.T, out_grad)
    return mixed, input_grad, gate_grad.T, up_grad.T, down_grad


def solution(mesh):
    return jax.shard_map(
        per_device,
        mesh=mesh,
        in_specs=(
            P("row", "col"), P("col", "row"), P("col", "row"), P("row", "col"), P(), P(), P(), P("row", "col"),
        ),
        out_specs=(P("row", "col"), P("row", "col"), P("col", "row"), P("col", "row"), P("row", "col")),
        check_vma=False,
    )
```

```python
import functools

import jax
import jax.numpy as jnp
from jax import lax
from jax.experimental import pallas as pl
from jax.experimental.pallas import tpu as pltpu
from jax.sharding import PartitionSpec as P

BLOCK = 128
NX, NY, NZ = 4, 4, 8
H = 32
NC = 2
T = H // NC
S = NX * T
NS = NC * NZ
FC = 512
F = 2 * FC
U = 448
UP = 512
W = 2 * U + UP
CUT = 640
DZ = (0, 1, -1, 2, -2, 3, -3, 4)
SLOT = {d % NZ: i for i, d in enumerate(DZ)}
GROUPS = ((0,), (1, 2), (3, 4), (5, 6), (7,))
ORDER = (
    "G0 A0 A1 G1",
    "M W B01 B00",
    "B10 B11 F00 F10",
    "N B02 F01 P01",
    "P00 P10 F11 B12",
    "Y01 B03 P11 F02",
    "Y10 Y00 P02 F12",
    "Y11 B13 P12 E00",
    "Y02 B04 F03 S00",
    "E11 P03 Y12 F13",
    "P13 B14 F04 P04",
    "E01 V00 Y03 Y04",
    "F14 P14 E12 Y13",
    "E04 S04 S01 X",
    "E02 Y14 E03 V04",
    "Q00 E10 S03 E13",
    "S13 E14 Q04 I00",
    "S14 I04 V03 S02",
    "Z04 V14 V13 V01",
    "Q03 I03 Z03 V02",
    "S12 S11 Q14 R04",
    "Z14 I14 Q13 I13",
    "Q02 I02 Z02 V11",
    "Z13 V12 Q01 I01",
    "S10 Z01 Q11 I11",
    "R00 V10 Q12 Z12",
    "I12 R01 Z00 R14",
    "Z11 Q10 R12 R13",
    "R03 R11 I10 Z10",
    "R10 R02",
)
BF = jnp.bfloat16
F32 = jnp.float32
MESH = pl.DeviceIdType.MESH


def nn(a, b):
    return jnp.dot(a, b, preferred_element_type=F32)


def nt(a, b):
    return lax.dot_general(a, b, (((1,), (1,)), ((), ())), preferred_element_type=F32)


def tn(a, b):
    return lax.dot_general(a, b, (((0,), (0,)), ((), ())), preferred_element_type=F32)


def kernel(
    tok, gw, uw, dw, gm, um, dm, og,
    mixed_o, ig_o, gg_o, ug_o, dg_o,
    ta, gb, to, go, gwo, uwo, dwo, wgu, kd, keep,
    pf, pp, ph, pr, hd, ho, mp, mz, mr, mr0, p2, ir, si, iz, sm, mx,
    s_ax, s_bz, s_w, s_bx, s_bh, s_az, s_rh, s_ry, s_ay, s_av, s_ho, s_to, s_mz, s_mzh, s_ix, s_iz, s_mx,
    r_ax, r_bz, r_w, r_bx, r_az, r_rh, r_ry, r_ay, r_av, r_ho, r_to, r_mz, r_ix, r_iz, r_mx,
):
    row, col = lax.axis_index("row"), lax.axis_index("col")
    z, x = row // NX, row % NX
    y, k = col // 2, col % 2

    def dev(dz, dx, dy, core):
        r = ((z + dz + NZ) % NZ) * NX + (x + dx) % NX
        return (r, ((y + dy) % NY) * 2 + core)

    sib = dev(0, 0, 0, 1 - k)

    def send(src, dst, ss, rs, to_dev):
        pltpu.make_async_remote_copy(
            src_ref=src, dst_ref=dst, send_sem=ss, recv_sem=rs, device_id=to_dev, device_id_type=MESH
        ).start()

    def local(src, dst, sem):
        pltpu.make_async_copy(src, dst, sem).start()

    def wait(ref, sem):
        pltpu.make_async_copy(ref, ref, sem).wait()

    def rows(start, size):
        return pl.ds(pl.multiple_of(start, 16), size)

    bar = pltpu.get_barrier_semaphore()
    partners = [sib]
    partners += [dev(0, e, 0, c) for e in range(1, NX) for c in (0, 1)]
    partners += [dev(e, 0, 0, c) for e in range(1, NZ) for c in (0, 1)]
    partners += [dev(0, 0, e, k) for e in range(1, NY)]
    for p in partners:
        pl.semaphore_signal(bar, inc=1, device_id=p, device_id_type=MESH)
    pl.semaphore_wait(bar, len(partners))

    def part_of(core, c):
        return rows(core * H + c * T, T)

    def block(c, s):
        return rows((c * NZ + s) * S + x * T, T)

    def start_tokens(c):
        mine = block(c, 0)
        for e in (1, 3, 2):
            for core in (0, 1):
                send(tok.at[part_of(core, c)], ta.at[k, mine], s_ax, r_ax.at[c], dev(0, e, 0, core))
        send(tok.at[part_of(1 - k, c)], ta.at[k, mine], s_ax, r_ax.at[c], sib)
        local(tok.at[part_of(k, c)], ta.at[k, mine], r_ax.at[c])

    def start_grads(c):
        send(og.at[part_of(1 - k, c)], gb.at[k, block(c, 0)], s_bz, r_bz.at[c, 0], sib)
        local(og.at[part_of(k, c)], gb.at[k, block(c, 0)], r_bz.at[c, 0])
        for e in (1, -1):
            t = SLOT[-e % NZ]
            for core in (0, 1):
                send(og.at[part_of(core, c)], gb.at[k, block(c, t)], s_bz, r_bz.at[c, t], dev(e, 0, 0, core))

    def forward_tokens(c, s):
        d = DZ[s]
        r = pl.ds((c * NZ + s) * S, S)
        if s == 0:
            wait(ta.at[:, r], r_ax.at[c])
        for j in (0, 1):
            if s:
                wait(ta.at[j, r], r_az.at[c, s, j])
            ahead = (1, -1) if s == 0 else (-1 if d > 0 else 1,)
            if s == 7 or (abs(d) == 3 and (d < 0) != (j == 1)):
                ahead = ()
            for e in ahead:
                t = SLOT[(d - e) % NZ]
                send(ta.at[j, r], ta.at[j, pl.ds((c * NZ + t) * S, S)], s_az.at[j], r_az.at[c, t, j], dev(e, 0, 0, k))

    def forward_grads(c, s):
        d = DZ[s]
        mine = block(c, s)
        wait(gb.at[:, pl.ds(0, T)], r_bz.at[c, s])
        e = -1 if d > 0 else 1
        if 0 < abs(d) < 4:
            t = SLOT[(d - e) % NZ]
            there = block(c, t)
            if abs(d) < 3:
                send(gb.at[:, mine], gb.at[:, there], s_bh.at[0], r_bz.at[c, t], dev(e, 0, 0, k))
            else:
                j = 0 if d < 0 else 1
                send(gb.at[j, mine], gb.at[j, there], s_bh.at[1], r_bz.at[c, t], dev(e, 0, 0, k))
        for e in (1, 3, 2):
            send(gb.at[:, mine], gb.at[:, mine], s_bx.at[e - 1], r_bx.at[c, s], dev(0, e, 0, k))

    def start_weights():
        send(gw, gwo, s_w.at[0], r_w.at[0], sib)
        send(uw, uwo, s_w.at[1], r_w.at[1], sib)
        send(dw, dwo, s_w.at[2], r_w.at[2], sib)

    def masks():
        unit = (row * U + lax.broadcasted_iota(jnp.int32, (U, 112), 0)) // BLOCK
        left = (unit == lax.broadcasted_iota(jnp.int32, (U, 112), 1)).astype(F32)
        feat = (y * F + lax.broadcasted_iota(jnp.int32, (32, F), 1)) // BLOCK
        right = (feat == lax.broadcasted_iota(jnp.int32, (32, F), 0)).astype(F32)
        for i, ref in enumerate((gm, um, dm)):
            keep[i] = nn(nt(left, ref[...].astype(F32)), right).astype(BF)

    def keep_weights(core, g_ref, u_ref, d_ref):
        c = pl.ds(pl.multiple_of(core * FC, FC), FC)
        wgu[0:U, c] = keep[0, :, c] * g_ref[...]
        wgu[U : 2 * U, c] = keep[1, :, c] * u_ref[...]
        kd[0:U, c] = keep[2, :, c] * d_ref[...]
        kd[U:UP, c] = jnp.zeros((UP - U, FC), BF)

    halves = (slice(0, CUT), slice(CUT, W))

    def stage1(c, slots):
        r = pl.ds((c * NZ + slots[0]) * S, len(slots) * S)
        for s in slots:
            wait(gb.at[:, pl.ds(0, 3 * T)], r_bx.at[c, s])
        both = nt(ta[0, r, :], wgu[:, 0:FC]) + nt(ta[1, r, :], wgu[:, FC:F])
        back = nt(gb[0, r, :], kd[:, 0:FC]) + nt(gb[1, r, :], kd[:, FC:F])
        pf[r, 0 : 2 * U] = both
        pf[r, 2 * U : W] = back
        pp[r, 0 : 2 * U] = both.astype(BF)
        pp[r, 2 * U : W] = back.astype(BF)
        for s in slots:
            g = c * NZ + s
            far = rows(g * S + (y + 2) % NY * T, T)
            for way, cols in enumerate(halves):
                send(pp.at[far, cols], ph.at[pl.ds(g * T, T), cols], s_rh.at[way], r_rh.at[c, s], dev(0, 0, 1 - 2 * way, k))

    def pass_sums(c, s):
        g = c * NZ + s
        r = pl.ds(g * T, T)
        wait(pp.at[pl.ds(0, T)], r_rh.at[c, s])
        for way, cols in enumerate(halves):
            there = rows(g * S + (y + 1 + 2 * way) % NY * T, T)
            pp[there, cols] = (pf[there, cols] + ph[r, cols].astype(F32)).astype(BF)
            send(pp.at[there], pr.at[way, r], s_ry.at[way], r_ry.at[c, s], dev(0, 0, 1 - 2 * way, k))

    def elementwise(c, s):
        g = c * NZ + s
        wait(pp.at[pl.ds(0, 2 * T)], r_ry.at[c, s])
        mine = rows(g * S + y * T, T)
        r = pl.ds(g * T, T)
        tot = pf[mine, :] + (pr[0, r, :].astype(F32) + pr[1, r, :].astype(F32))
        gate, up, hg = tot[:, 0:U], tot[:, U : 2 * U], tot[:, 2 * U : 3 * U]
        sig = 1.0 / (1.0 + jnp.exp(-gate))
        act = gate * sig
        dgate = hg * up * sig * (1.0 + gate * (1.0 - sig))
        dup = hg * act
        hd[mine, :] = jnp.concatenate([dgate, dup, act * up, jnp.zeros((T, UP - U), F32)], axis=1).astype(BF)

    def share(c, s):
        g = c * NZ + s
        mine = rows(g * S + y * T, T)
        for way in (0, 1):
            send(hd.at[mine], hd.at[mine], s_ay.at[way], r_ay.at[c, s, way], dev(0, 0, 1 - 2 * way, k))

    def share_on(c, s):
        g = c * NZ + s
        for way, cols in enumerate(halves):
            there = rows(g * S + (y + 3 - 2 * way) % NY * T, T)
            wait(hd.at[there], r_ay.at[c, s, way])
            send(hd.at[there, cols], hd.at[there, cols], s_av.at[way], r_av.at[c, s], dev(0, 0, 1 - 2 * way, k))

    def stage2(c, slots):
        r = pl.ds((c * NZ + slots[0]) * S, len(slots) * S)
        for s in slots:
            wait(hd.at[pl.ds(0, T)], r_av.at[c, s])
        mp[r, :] = nn(hd[r, 2 * U : W], kd[...])
        p2[r, :] = nn(hd[r, 0 : 2 * U], wgu[...]).astype(BF)
        send(hd.at[r], ho.at[r], s_ho, r_ho, sib)

    def send_inputs(c, s):
        g = c * NZ + s
        for e in (1, 3, 2):
            other = (x + e) % NX
            send(p2.at[rows(g * S + other * T, T)], ir.at[e - 1, pl.ds(g * T, T)], s_ix.at[e - 1], r_ix.at[c, s], dev(0, e, 0, k))

    def pass_mixed(c, s):
        d = DZ[s]
        r = pl.ds((c * NZ + s) * S, S)
        way = 0 if d < 0 else 1
        ahead = dev(-1 if d < 0 else 1, 0, 0, k)
        if s == 7:
            mz[r, :] = mp[r, :].astype(BF)
            for way, t in ((0, 6), (1, 5)):
                half = slice(way * FC, (way + 1) * FC)
                there = pl.ds((c * NZ + t) * S, S)
                send(mz.at[r, half], mr.at[there, half], s_mzh.at[way], r_mz.at[c, t], dev(2 * way - 1, 0, 0, k))
        elif s:
            if abs(d) == 3:
                half = slice(way * FC, (way + 1) * FC)
                rest = slice((1 - way) * FC, (2 - way) * FC)
                mz[r, rest] = mp[r, rest].astype(BF)
                wait(mr.at[r, half], r_mz.at[c, s])
                mz[r, half] = (mp[r, half] + mr[r, half].astype(F32)).astype(BF)
            else:
                wait(mr.at[r], r_mz.at[c, s])
                mz[r, :] = (mp[r, :] + mr[r, :].astype(F32)).astype(BF)
            if abs(d) == 1:
                send(mz.at[r], mr0.at[c, way], s_mz.at[way], r_mz.at[c, 7 * way], ahead)
            else:
                t = s - 2
                send(mz.at[r], mr.at[pl.ds((c * NZ + t) * S, S)], s_mz.at[way], r_mz.at[c, t], ahead)
        else:
            wait(mr0.at[c, 0], r_mz.at[c, 0])
            wait(mr0.at[c, 1], r_mz.at[c, 7])
            tot = mp[r, :] + (mr0[c, 0].astype(F32) + mr0[c, 1].astype(F32))
            sm[c, 0] = tot[:, 0:FC]
            sm[c, 1] = tot[:, FC:F]
            mine = rows(x * T, T)
            for e in (1, 3, 2):
                other = rows((x + e) % NX * T, T)
                for core in (0, 1):
                    send(sm.at[c, core, other], mx.at[c, k, mine], s_mx, r_mx.at[c], dev(0, e, 0, core))
            send(sm.at[c, 1 - k, mine], mx.at[c, k, mine], s_mx, r_mx.at[c], sib)
            local(sm.at[c, k, mine], mx.at[c, k, mine], r_mx.at[c])

    def reduce_inputs(c, s):
        d = DZ[s]
        g = c * NZ + s
        wait(p2.at[pl.ds(0, 3 * T)], r_ix.at[c, s])
        r = pl.ds(g * T, T)
        own = p2[rows(g * S + x * T, T), :].astype(F32)
        tot = ((own + ir[0, r, :].astype(F32)) + (ir[1, r, :].astype(F32) + ir[2, r, :].astype(F32))).astype(BF)
        si[0, r, :] = tot[:, 0:FC]
        si[1, r, :] = tot[:, FC:F]
        t = pl.ds((c * NZ + SLOT[-d % NZ]) * T, T)
        if s:
            for core in (0, 1):
                send(si.at[core, r], iz.at[k, t], s_iz, r_iz.at[c], dev(d, 0, 0, core))
        else:
            send(si.at[1 - k, r], iz.at[k, t], s_iz, r_iz.at[c], sib)
            local(si.at[k, r], iz.at[k, t], r_iz.at[c])

    def each(step, c, g):
        for s in GROUPS[g]:
            step(c, s)

    def finish_weights():
        wait(gwo, r_w.at[0])
        wait(uwo, r_w.at[1])
        wait(dwo, r_w.at[2])
        keep_weights(1 - k, gwo, uwo, dwo)

    def swap_inputs():
        send(ta.at[1 - k], to, s_to.at[0], r_to.at[0], sib)
        send(gb.at[1 - k], go, s_to.at[1], r_to.at[1], sib)

    def begin():
        masks()
        keep_weights(k, gw, uw, dw)

    steps = {
        "A": start_tokens,
        "G": start_grads,
        "F": lambda c, g: each(forward_tokens, c, g),
        "B": lambda c, g: each(forward_grads, c, g),
        "P": lambda c, g: stage1(c, GROUPS[g]),
        "Y": lambda c, g: each(pass_sums, c, g),
        "V": lambda c, g: each(share_on, c, g),
        "E": lambda c, g: each(elementwise, c, g),
        "S": lambda c, g: each(share, c, g),
        "Q": lambda c, g: stage2(c, GROUPS[g]),
        "I": lambda c, g: each(send_inputs, c, g),
        "Z": lambda c, g: each(pass_mixed, c, g),
        "R": lambda c, g: each(reduce_inputs, c, g),
        "W": start_weights,
        "M": begin,
        "N": finish_weights,
        "X": swap_inputs,
    }
    for line in ORDER:
        for step in line.split():
            steps[step[0]](*map(int, step[1:]))

    wait(to, r_to.at[0])
    wait(go, r_to.at[1])
    wait(ho, r_ho)
    own = pl.ds(pl.multiple_of(k * FC, FC), FC)
    for i, out in enumerate((gg_o, ug_o)):
        c = slice(i * U, (i + 1) * U)
        out[...] = (tn(hd[:, c], ta[k]) + tn(ho[:, c], to[...])) * keep[i, :, own].astype(F32)
    c = slice(2 * U, 3 * U)
    dg_o[...] = (tn(hd[:, c], gb[k]) + tn(ho[:, c], go[...])) * keep[2, :, own].astype(F32)

    for c in range(NC):
        wait(mx.at[c], r_mx.at[c])
        for core in (0, 1):
            part = [mx[c, core, i * T : (i + 1) * T, :] for i in range(NX)]
            there = slice(core * H + c * T, core * H + (c + 1) * T)
            mixed_o[there, :] = ((part[0] + part[1]) + (part[2] + part[3])).astype(BF)
    for c in range(NC):
        wait(iz.at[:, pl.ds(c * NZ * T, NZ * T)], r_iz.at[c])
        for core in (0, 1):
            part = [iz[core, (c * NZ + i) * T : (c * NZ + i + 1) * T, :].astype(F32) for i in range(NZ)]
            low = (part[0] + part[1]) + (part[2] + part[3])
            high = (part[4] + part[5]) + (part[6] + part[7])
            there = slice(core * H + c * T, core * H + (c + 1) * T)
            ig_o[there, :] = (low + high).astype(BF)

    wait(ta.at[0, pl.ds(0, 7 * NC * T)], s_ax)
    wait(ta.at[0, pl.ds(0, 5 * NC * T)], s_bz)
    wait(gb.at[:, pl.ds(0, 4 * NC * T)], s_bh.at[0])
    wait(gb.at[0, pl.ds(0, 2 * NC * T)], s_bh.at[1])
    for i in range(3):
        wait((gwo, uwo, dwo)[i], s_w.at[i])
        wait(gb.at[:, pl.ds(0, NS * T)], s_bx.at[i])
        wait(p2.at[pl.ds(0, NS * T)], s_ix.at[i])
    for j in (0, 1):
        wait(ta.at[j, pl.ds(0, 7 * NC * S)], s_az.at[j])
        wait(pp.at[pl.ds(0, NS * T)], s_ry.at[j])
        wait(hd.at[pl.ds(0, NS * T)], s_ay.at[j])
        wait(pp.at[pl.ds(0, NS * T), halves[j]], s_rh.at[j])
        wait(hd.at[pl.ds(0, NS * T), halves[j]], s_av.at[j])
        wait(to, s_to.at[j])
        wait(mz.at[pl.ds(0, 3 * NC * S)], s_mz.at[j])
        wait(mz.at[pl.ds(0, NC * S), 0:FC], s_mzh.at[j])
    wait(ho, s_ho)
    wait(gb.at[0, pl.ds(0, 15 * NC * T)], s_iz)
    wait(ta.at[:, pl.ds(0, 7 * NC * T)], s_mx)


def per_device(tokens, gate_weight, up_weight, down_weight, gate_mask, up_mask, down_mask, out_grad):
    vmem = pl.BlockSpec(memory_space=pltpu.VMEM)
    dma = pltpu.SemaphoreType.DMA
    v = pltpu.VMEM
    mixed, input_grad, gate_grad, up_grad, down_grad = pl.pallas_call(
        kernel,
        out_shape=(
            jax.ShapeDtypeStruct((2 * H, FC), BF),
            jax.ShapeDtypeStruct((2 * H, FC), BF),
            jax.ShapeDtypeStruct((U, FC), F32),
            jax.ShapeDtypeStruct((U, FC), F32),
            jax.ShapeDtypeStruct((U, FC), F32),
        ),
        in_specs=[vmem] * 8,
        out_specs=(vmem,) * 5,
        scratch_shapes=[
            v((2, NS * S, FC), BF),
            v((2, NS * S, FC), BF),
            v((NS * S, FC), BF),
            v((NS * S, FC), BF),
            v((U, FC), BF),
            v((U, FC), BF),
            v((U, FC), BF),
            v((2 * U, F), BF),
            v((UP, F), BF),
            v((3, U, F), BF),
            v((NS * S, W), F32),
            v((NS * S, W), BF),
            v((NS * T, W), BF),
            v((2, NS * T, W), BF),
            v((NS * S, W), BF),
            v((NS * S, W), BF),
            v((NS * S, F), F32),
            v((NS * S, F), BF),
            v((NS * S, F), BF),
            v((NC, 2, S, F), BF),
            v((NS * S, F), BF),
            v((3, NS * T, F), BF),
            v((2, NS * T, FC), BF),
            v((2, NS * T, FC), BF),
            v((NC, 2, S, FC), F32),
            v((NC, 2, S, FC), F32),
            dma, dma, dma((3,)), dma((3,)), dma((2,)), dma((2,)), dma((2,)), dma((2,)), dma((2,)), dma((2,)), dma, dma((2,)), dma((2,)), dma((2,)), dma((3,)), dma, dma,
            dma((NC,)), dma((NC, 8)), dma((3,)), dma((NC, 8)), dma((NC, 8, 2)), dma((NC, 8)), dma((NC, 8)), dma((NC, 8, 2)), dma((NC, 8)), dma, dma((2,)), dma((NC, 8)), dma((NC, 8)), dma((NC,)), dma((NC,)),
        ],
        compiler_params=pltpu.CompilerParams(
            collective_id=0, has_side_effects=True, vmem_limit_bytes=60 << 20
        ),
        cost_estimate=pl.CostEstimate(flops=9_000_000_000, bytes_accessed=8 << 20, transcendentals=120_000),
        name="sublayer",
    )(tokens, gate_weight.T, up_weight.T, down_weight, gate_mask, up_mask, down_mask.T, out_grad)
    return mixed, input_grad, gate_grad.T, up_grad.T, down_grad


def solution(mesh):
    return jax.shard_map(
        per_device,
        mesh=mesh,
        in_specs=(
            P("row", "col"), P("col", "row"), P("col", "row"), P("row", "col"), P(), P(), P(), P("row", "col"),
        ),
        out_specs=(P("row", "col"), P("row", "col"), P("col", "row"), P("col", "row"), P("row", "col")),
        check_vma=False,
    )
```

```python
import functools

import jax
import jax.numpy as jnp
from jax import lax
from jax.experimental import pallas as pl
from jax.experimental.pallas import tpu as pltpu
from jax.sharding import PartitionSpec as P

BLOCK = 128
NX, NY, NZ = 4, 4, 8
H = 32
NC = 2
T = H // NC
S = NX * T
NS = NC * NZ
FC = 512
F = 2 * FC
U = 448
UP = 512
W = 2 * U + UP
CUT = 640
DZ = (0, 1, -1, 2, -2, 3, -3, 4)
SLOT = {d % NZ: i for i, d in enumerate(DZ)}
GROUPS = ((0,), (1, 2), (3, 4), (5, 6), (7,))
ORDER = (
    "A0 G0 A1 G1",
    "B10 W B01 B11",
    "F00 M F10 B02",
    "N P10 F01 P01",
    "B12 F11 Y10 P11",
    "B03 Y01 E10 S10",
    "F02 P02 Y11 F12",
    "V10 P12 B04 B13",
    "Y02 F03 P03 Y12",
    "F13 E02 B00 S02",
    "B14 F04 E01 P04",
    "Y03 F14 P13 V02",
    "E12 P14 Q10 Y04",
    "Y13 E03 Y14 E04",
    "S04 S03 E14 S14",
    "V04 E13 S13 Q02",
    "I10 I02 V14 V03",
    "P00 Q04 Z04 S01",
    "I04 Q14 I14 Z14",
    "V13 Q03 I03 S12",
    "Y00 Z03 V01 E11",
    "Q13 Z13 V12 I13",
    "S11 E00 S00 Z02",
    "Q01 R10 I01 Q12",
    "Z12 V11 I12 V00",
    "Z01 Q11 I11 R14",
    "X Z11 Q00 R13",
    "I00 R04 R03 R12",
    "R02 R01 Z00 Z10",
    "R00 R11",
)
BF = jnp.bfloat16
F32 = jnp.float32
MESH = pl.DeviceIdType.MESH


def nn(a, b):
    return jnp.dot(a, b, preferred_element_type=F32)


def nt(a, b):
    return lax.dot_general(a, b, (((1,), (1,)), ((), ())), preferred_element_type=F32)


def tn(a, b):
    return lax.dot_general(a, b, (((0,), (0,)), ((), ())), preferred_element_type=F32)


def kernel(
    tok, gw, uw, dw, gm, um, dm, og,
    mixed_o, ig_o, gg_o, ug_o, dg_o,
    ta, gb, to, go, gwo, uwo, dwo, wgu, kd, keep,
    pf, pp, ph, pr, hd, ho, mp, mz, mr, mr0, p2, ir, si, iz, sm, mx,
    s_ax, s_bz, s_w, s_bx, s_bh, s_az, s_rh, s_ry, s_ay, s_av, s_ho, s_to, s_mz, s_mzh, s_ix, s_iz, s_mx,
    r_ax, r_bz, r_w, r_bx, r_az, r_rh, r_ry, r_ay, r_av, r_ho, r_to, r_mz, r_ix, r_iz, r_mx,
):
    row, col = lax.axis_index("row"), lax.axis_index("col")
    z, x = row // NX, row % NX
    y, k = col // 2, col % 2

    def dev(dz, dx, dy, core):
        r = ((z + dz + NZ) % NZ) * NX + (x + dx) % NX
        return (r, ((y + dy) % NY) * 2 + core)

    sib = dev(0, 0, 0, 1 - k)

    def send(src, dst, ss, rs, to_dev):
        pltpu.make_async_remote_copy(
            src_ref=src, dst_ref=dst, send_sem=ss, recv_sem=rs, device_id=to_dev, device_id_type=MESH
        ).start()

    def local(src, dst, sem):
        pltpu.make_async_copy(src, dst, sem).start()

    def wait(ref, sem):
        pltpu.make_async_copy(ref, ref, sem).wait()

    def rows(start, size):
        return pl.ds(pl.multiple_of(start, 16), size)

    bar = pltpu.get_barrier_semaphore()
    partners = [sib]
    partners += [dev(0, e, 0, c) for e in range(1, NX) for c in (0, 1)]
    partners += [dev(e, 0, 0, c) for e in range(1, NZ) for c in (0, 1)]
    partners += [dev(0, 0, e, k) for e in range(1, NY)]
    for p in partners:
        pl.semaphore_signal(bar, inc=1, device_id=p, device_id_type=MESH)
    pl.semaphore_wait(bar, len(partners))

    def part_of(core, c):
        return rows(core * H + c * T, T)

    def block(c, s):
        return rows((c * NZ + s) * S + x * T, T)

    def start_tokens(c):
        mine = block(c, 0)
        for e in (1, 3, 2):
            for core in (0, 1):
                send(tok.at[part_of(core, c)], ta.at[k, mine], s_ax, r_ax.at[c], dev(0, e, 0, core))
        send(tok.at[part_of(1 - k, c)], ta.at[k, mine], s_ax, r_ax.at[c], sib)
        local(tok.at[part_of(k, c)], ta.at[k, mine], r_ax.at[c])

    def start_grads(c):
        send(og.at[part_of(1 - k, c)], gb.at[k, block(c, 0)], s_bz, r_bz.at[c, 0], sib)
        local(og.at[part_of(k, c)], gb.at[k, block(c, 0)], r_bz.at[c, 0])
        for e in (1, -1):
            t = SLOT[-e % NZ]
            for core in (0, 1):
                send(og.at[part_of(core, c)], gb.at[k, block(c, t)], s_bz, r_bz.at[c, t], dev(e, 0, 0, core))

    def forward_tokens(c, s):
        d = DZ[s]
        r = pl.ds((c * NZ + s) * S, S)
        if s == 0:
            wait(ta.at[:, r], r_ax.at[c])
        for j in (0, 1):
            if s:
                wait(ta.at[j, r], r_az.at[c, s, j])
            ahead = (1, -1) if s == 0 else (-1 if d > 0 else 1,)
            if s == 7 or (abs(d) == 3 and (d < 0) != (j == 1)):
                ahead = ()
            for e in ahead:
                t = SLOT[(d - e) % NZ]
                send(ta.at[j, r], ta.at[j, pl.ds((c * NZ + t) * S, S)], s_az.at[j], r_az.at[c, t, j], dev(e, 0, 0, k))

    def forward_grads(c, s):
        d = DZ[s]
        mine = block(c, s)
        wait(gb.at[:, pl.ds(0, T)], r_bz.at[c, s])
        e = -1 if d > 0 else 1
        if 0 < abs(d) < 4:
            t = SLOT[(d - e) % NZ]
            there = block(c, t)
            if abs(d) < 3:
                send(gb.at[:, mine], gb.at[:, there], s_bh.at[0], r_bz.at[c, t], dev(e, 0, 0, k))
            else:
                j = 0 if d < 0 else 1
                send(gb.at[j, mine], gb.at[j, there], s_bh.at[1], r_bz.at[c, t], dev(e, 0, 0, k))
        for e in (1, 3, 2):
            send(gb.at[:, mine], gb.at[:, mine], s_bx.at[e - 1], r_bx.at[c, s], dev(0, e, 0, k))

    def start_weights():
        send(gw, gwo, s_w.at[0], r_w.at[0], sib)
        send(uw, uwo, s_w.at[1], r_w.at[1], sib)
        send(dw, dwo, s_w.at[2], r_w.at[2], sib)

    def masks():
        unit = (row * U + lax.broadcasted_iota(jnp.int32, (U, 112), 0)) // BLOCK
        left = (unit == lax.broadcasted_iota(jnp.int32, (U, 112), 1)).astype(F32)
        feat = (y * F + lax.broadcasted_iota(jnp.int32, (32, F), 1)) // BLOCK
        right = (feat == lax.broadcasted_iota(jnp.int32, (32, F), 0)).astype(F32)
        for i, ref in enumerate((gm, um, dm)):
            keep[i] = nn(nt(left, ref[...].astype(F32)), right).astype(BF)

    def keep_weights(core, g_ref, u_ref, d_ref):
        c = pl.ds(pl.multiple_of(core * FC, FC), FC)
        wgu[0:U, c] = keep[0, :, c] * g_ref[...]
        wgu[U : 2 * U, c] = keep[1, :, c] * u_ref[...]
        kd[0:U, c] = keep[2, :, c] * d_ref[...]
        kd[U:UP, c] = jnp.zeros((UP - U, FC), BF)

    halves = (slice(0, CUT), slice(CUT, W))

    def stage1(c, slots):
        r = pl.ds((c * NZ + slots[0]) * S, len(slots) * S)
        for s in slots:
            wait(gb.at[:, pl.ds(0, 3 * T)], r_bx.at[c, s])
        both = nt(ta[0, r, :], wgu[:, 0:FC]) + nt(ta[1, r, :], wgu[:, FC:F])
        back = nt(gb[0, r, :], kd[:, 0:FC]) + nt(gb[1, r, :], kd[:, FC:F])
        pf[r, 0 : 2 * U] = both
        pf[r, 2 * U : W] = back
        pp[r, 0 : 2 * U] = both.astype(BF)
        pp[r, 2 * U : W] = back.astype(BF)
        for s in slots:
            g = c * NZ + s
            far = rows(g * S + (y + 2) % NY * T, T)
            for way, cols in enumerate(halves):
                send(pp.at[far, cols], ph.at[pl.ds(g * T, T), cols], s_rh.at[way], r_rh.at[c, s], dev(0, 0, 1 - 2 * way, k))

    def pass_sums(c, s):
        g = c * NZ + s
        r = pl.ds(g * T, T)
        wait(pp.at[pl.ds(0, T)], r_rh.at[c, s])
        for way, cols in enumerate(halves):
            there = rows(g * S + (y + 1 + 2 * way) % NY * T, T)
            pp[there, cols] = (pf[there, cols] + ph[r, cols].astype(F32)).astype(BF)
            send(pp.at[there], pr.at[way, r], s_ry.at[way], r_ry.at[c, s], dev(0, 0, 1 - 2 * way, k))

    def elementwise(c, s):
        g = c * NZ + s
        wait(pp.at[pl.ds(0, 2 * T)], r_ry.at[c, s])
        mine = rows(g * S + y * T, T)
        r = pl.ds(g * T, T)
        tot = pf[mine, :] + (pr[0, r, :].astype(F32) + pr[1, r, :].astype(F32))
        gate, up, hg = tot[:, 0:U], tot[:, U : 2 * U], tot[:, 2 * U : 3 * U]
        sig = 1.0 / (1.0 + jnp.exp(-gate))
        act = gate * sig
        dgate = hg * up * sig * (1.0 + gate * (1.0 - sig))
        dup = hg * act
        hd[mine, :] = jnp.concatenate([dgate, dup, act * up, jnp.zeros((T, UP - U), F32)], axis=1).astype(BF)

    def share(c, s):
        g = c * NZ + s
        mine = rows(g * S + y * T, T)
        for way in (0, 1):
            send(hd.at[mine], hd.at[mine], s_ay.at[way], r_ay.at[c, s, way], dev(0, 0, 1 - 2 * way, k))

    def share_on(c, s):
        g = c * NZ + s
        for way, cols in enumerate(halves):
            there = rows(g * S + (y + 3 - 2 * way) % NY * T, T)
            wait(hd.at[there], r_ay.at[c, s, way])
            send(hd.at[there, cols], hd.at[there, cols], s_av.at[way], r_av.at[c, s], dev(0, 0, 1 - 2 * way, k))

    def stage2(c, slots):
        r = pl.ds((c * NZ + slots[0]) * S, len(slots) * S)
        for s in slots:
            wait(hd.at[pl.ds(0, T)], r_av.at[c, s])
        mp[r, :] = nn(hd[r, 2 * U : W], kd[...])
        p2[r, :] = nn(hd[r, 0 : 2 * U], wgu[...]).astype(BF)
        send(hd.at[r], ho.at[r], s_ho, r_ho, sib)

    def send_inputs(c, s):
        g = c * NZ + s
        for e in (1, 3, 2):
            other = (x + e) % NX
            send(p2.at[rows(g * S + other * T, T)], ir.at[e - 1, pl.ds(g * T, T)], s_ix.at[e - 1], r_ix.at[c, s], dev(0, e, 0, k))

    def pass_mixed(c, s):
        d = DZ[s]
        r = pl.ds((c * NZ + s) * S, S)
        way = 0 if d < 0 else 1
        ahead = dev(-1 if d < 0 else 1, 0, 0, k)
        if s == 7:
            mz[r, :] = mp[r, :].astype(BF)
            for way, t in ((0, 6), (1, 5)):
                half = slice(way * FC, (way + 1) * FC)
                there = pl.ds((c * NZ + t) * S, S)
                send(mz.at[r, half], mr.at[there, half], s_mzh.at[way], r_mz.at[c, t], dev(2 * way - 1, 0, 0, k))
        elif s:
            if abs(d) == 3:
                half = slice(way * FC, (way + 1) * FC)
                rest = slice((1 - way) * FC, (2 - way) * FC)
                mz[r, rest] = mp[r, rest].astype(BF)
                wait(mr.at[r, half], r_mz.at[c, s])
                mz[r, half] = (mp[r, half] + mr[r, half].astype(F32)).astype(BF)
            else:
                wait(mr.at[r], r_mz.at[c, s])
                mz[r, :] = (mp[r, :] + mr[r, :].astype(F32)).astype(BF)
            if abs(d) == 1:
                send(mz.at[r], mr0.at[c, way], s_mz.at[way], r_mz.at[c, 7 * way], ahead)
            else:
                t = s - 2
                send(mz.at[r], mr.at[pl.ds((c * NZ + t) * S, S)], s_mz.at[way], r_mz.at[c, t], ahead)
        else:
            wait(mr0.at[c, 0], r_mz.at[c, 0])
            wait(mr0.at[c, 1], r_mz.at[c, 7])
            tot = mp[r, :] + (mr0[c, 0].astype(F32) + mr0[c, 1].astype(F32))
            sm[c, 0] = tot[:, 0:FC]
            sm[c, 1] = tot[:, FC:F]
            mine = rows(x * T, T)
            for e in (1, 3, 2):
                other = rows((x + e) % NX * T, T)
                for core in (0, 1):
                    send(sm.at[c, core, other], mx.at[c, k, mine], s_mx, r_mx.at[c], dev(0, e, 0, core))
            send(sm.at[c, 1 - k, mine], mx.at[c, k, mine], s_mx, r_mx.at[c], sib)
            local(sm.at[c, k, mine], mx.at[c, k, mine], r_mx.at[c])

    def reduce_inputs(c, s):
        d = DZ[s]
        g = c * NZ + s
        wait(p2.at[pl.ds(0, 3 * T)], r_ix.at[c, s])
        r = pl.ds(g * T, T)
        own = p2[rows(g * S + x * T, T), :].astype(F32)
        tot = ((own + ir[0, r, :].astype(F32)) + (ir[1, r, :].astype(F32) + ir[2, r, :].astype(F32))).astype(BF)
        si[0, r, :] = tot[:, 0:FC]
        si[1, r, :] = tot[:, FC:F]
        t = pl.ds((c * NZ + SLOT[-d % NZ]) * T, T)
        if s:
            for core in (0, 1):
                send(si.at[core, r], iz.at[k, t], s_iz, r_iz.at[c], dev(d, 0, 0, core))
        else:
            send(si.at[1 - k, r], iz.at[k, t], s_iz, r_iz.at[c], sib)
            local(si.at[k, r], iz.at[k, t], r_iz.at[c])

    def each(step, c, g):
        for s in GROUPS[g]:
            step(c, s)

    def finish_weights():
        wait(gwo, r_w.at[0])
        wait(uwo, r_w.at[1])
        wait(dwo, r_w.at[2])
        keep_weights(1 - k, gwo, uwo, dwo)

    def swap_inputs():
        send(ta.at[1 - k], to, s_to.at[0], r_to.at[0], sib)
        send(gb.at[1 - k], go, s_to.at[1], r_to.at[1], sib)

    def begin():
        masks()
        keep_weights(k, gw, uw, dw)

    steps = {
        "A": start_tokens,
        "G": start_grads,
        "F": lambda c, g: each(forward_tokens, c, g),
        "B": lambda c, g: each(forward_grads, c, g),
        "P": lambda c, g: stage1(c, GROUPS[g]),
        "Y": lambda c, g: each(pass_sums, c, g),
        "V": lambda c, g: each(share_on, c, g),
        "E": lambda c, g: each(elementwise, c, g),
        "S": lambda c, g: each(share, c, g),
        "Q": lambda c, g: stage2(c, GROUPS[g]),
        "I": lambda c, g: each(send_inputs, c, g),
        "Z": lambda c, g: each(pass_mixed, c, g),
        "R": lambda c, g: each(reduce_inputs, c, g),
        "W": start_weights,
        "M": begin,
        "N": finish_weights,
        "X": swap_inputs,
    }
    for line in ORDER:
        for step in line.split():
            steps[step[0]](*map(int, step[1:]))

    wait(to, r_to.at[0])
    wait(go, r_to.at[1])
    wait(ho, r_ho)
    own = pl.ds(pl.multiple_of(k * FC, FC), FC)
    for i, out in enumerate((gg_o, ug_o)):
        c = slice(i * U, (i + 1) * U)
        out[...] = (tn(hd[:, c], ta[k]) + tn(ho[:, c], to[...])) * keep[i, :, own].astype(F32)
    c = slice(2 * U, 3 * U)
    dg_o[...] = (tn(hd[:, c], gb[k]) + tn(ho[:, c], go[...])) * keep[2, :, own].astype(F32)

    for c in range(NC):
        wait(mx.at[c], r_mx.at[c])
        for core in (0, 1):
            part = [mx[c, core, i * T : (i + 1) * T, :] for i in range(NX)]
            there = slice(core * H + c * T, core * H + (c + 1) * T)
            mixed_o[there, :] = ((part[0] + part[1]) + (part[2] + part[3])).astype(BF)
    for c in range(NC):
        wait(iz.at[:, pl.ds(c * NZ * T, NZ * T)], r_iz.at[c])
        for core in (0, 1):
            part = [iz[core, (c * NZ + i) * T : (c * NZ + i + 1) * T, :].astype(F32) for i in range(NZ)]
            low = (part[0] + part[1]) + (part[2] + part[3])
            high = (part[4] + part[5]) + (part[6] + part[7])
            there = slice(core * H + c * T, core * H + (c + 1) * T)
            ig_o[there, :] = (low + high).astype(BF)

    wait(ta.at[0, pl.ds(0, 7 * NC * T)], s_ax)
    wait(ta.at[0, pl.ds(0, 5 * NC * T)], s_bz)
    wait(gb.at[:, pl.ds(0, 4 * NC * T)], s_bh.at[0])
    wait(gb.at[0, pl.ds(0, 2 * NC * T)], s_bh.at[1])
    for i in range(3):
        wait((gwo, uwo, dwo)[i], s_w.at[i])
        wait(gb.at[:, pl.ds(0, NS * T)], s_bx.at[i])
        wait(p2.at[pl.ds(0, NS * T)], s_ix.at[i])
    for j in (0, 1):
        wait(ta.at[j, pl.ds(0, 7 * NC * S)], s_az.at[j])
        wait(pp.at[pl.ds(0, NS * T)], s_ry.at[j])
        wait(hd.at[pl.ds(0, NS * T)], s_ay.at[j])
        wait(pp.at[pl.ds(0, NS * T), halves[j]], s_rh.at[j])
        wait(hd.at[pl.ds(0, NS * T), halves[j]], s_av.at[j])
        wait(to, s_to.at[j])
        wait(mz.at[pl.ds(0, 3 * NC * S)], s_mz.at[j])
        wait(mz.at[pl.ds(0, NC * S), 0:FC], s_mzh.at[j])
    wait(ho, s_ho)
    wait(gb.at[0, pl.ds(0, 15 * NC * T)], s_iz)
    wait(ta.at[:, pl.ds(0, 7 * NC * T)], s_mx)


def per_device(tokens, gate_weight, up_weight, down_weight, gate_mask, up_mask, down_mask, out_grad):
    vmem = pl.BlockSpec(memory_space=pltpu.VMEM)
    dma = pltpu.SemaphoreType.DMA
    v = pltpu.VMEM
    mixed, input_grad, gate_grad, up_grad, down_grad = pl.pallas_call(
        kernel,
        out_shape=(
            jax.ShapeDtypeStruct((2 * H, FC), BF),
            jax.ShapeDtypeStruct((2 * H, FC), BF),
            jax.ShapeDtypeStruct((U, FC), F32),
            jax.ShapeDtypeStruct((U, FC), F32),
            jax.ShapeDtypeStruct((U, FC), F32),
        ),
        in_specs=[vmem] * 8,
        out_specs=(vmem,) * 5,
        scratch_shapes=[
            v((2, NS * S, FC), BF),
            v((2, NS * S, FC), BF),
            v((NS * S, FC), BF),
            v((NS * S, FC), BF),
            v((U, FC), BF),
            v((U, FC), BF),
            v((U, FC), BF),
            v((2 * U, F), BF),
            v((UP, F), BF),
            v((3, U, F), BF),
            v((NS * S, W), F32),
            v((NS * S, W), BF),
            v((NS * T, W), BF),
            v((2, NS * T, W), BF),
            v((NS * S, W), BF),
            v((NS * S, W), BF),
            v((NS * S, F), F32),
            v((NS * S, F), BF),
            v((NS * S, F), BF),
            v((NC, 2, S, F), BF),
            v((NS * S, F), BF),
            v((3, NS * T, F), BF),
            v((2, NS * T, FC), BF),
            v((2, NS * T, FC), BF),
            v((NC, 2, S, FC), F32),
            v((NC, 2, S, FC), F32),
            dma, dma, dma((3,)), dma((3,)), dma((2,)), dma((2,)), dma((2,)), dma((2,)), dma((2,)), dma((2,)), dma, dma((2,)), dma((2,)), dma((2,)), dma((3,)), dma, dma,
            dma((NC,)), dma((NC, 8)), dma((3,)), dma((NC, 8)), dma((NC, 8, 2)), dma((NC, 8)), dma((NC, 8)), dma((NC, 8, 2)), dma((NC, 8)), dma, dma((2,)), dma((NC, 8)), dma((NC, 8)), dma((NC,)), dma((NC,)),
        ],
        compiler_params=pltpu.CompilerParams(
            collective_id=0, has_side_effects=True, vmem_limit_bytes=60 << 20
        ),
        cost_estimate=pl.CostEstimate(flops=9_000_000_000, bytes_accessed=8 << 20, transcendentals=120_000),
        name="sublayer",
    )(tokens, gate_weight.T, up_weight.T, down_weight, gate_mask, up_mask, down_mask.T, out_grad)
    return mixed, input_grad, gate_grad.T, up_grad.T, down_grad


def solution(mesh):
    return jax.shard_map(
        per_device,
        mesh=mesh,
        in_specs=(
            P("row", "col"), P("col", "row"), P("col", "row"), P("row", "col"), P(), P(), P(), P("row", "col"),
        ),
        out_specs=(P("row", "col"), P("row", "col"), P("col", "row"), P("col", "row"), P("row", "col")),
        check_vma=False,
    )
```

```python
import functools

import jax
import jax.numpy as jnp
from jax import lax
from jax.experimental import pallas as pl
from jax.experimental.pallas import tpu as pltpu
from jax.sharding import PartitionSpec as P

BLOCK = 128
NX, NY, NZ = 4, 4, 8
H = 32
NC = 2
T = H // NC
S = NX * T
NS = NC * NZ
FC = 512
F = 2 * FC
U = 448
UP = 512
W = 2 * U + UP
CUT = 640
DZ = (0, 1, -1, 2, -2, 3, -3, 4)
SLOT = {d % NZ: i for i, d in enumerate(DZ)}
GROUPS = ((0,), (1, 2), (3, 4), (5, 6), (7,))
ORDER = (
    "A0 G0 A1 G1",
    "B10 W B01 B11",
    "F00 M F10 B02",
    "N P10 F01 P01",
    "B12 F11 Y10 P11",
    "B03 Y01 E10 S10",
    "F02 P02 Y11 F12",
    "V10 P12 B04 B13",
    "Y02 F03 P03 Y12",
    "F13 E02 B00 S02",
    "B14 F04 E01 P04",
    "Y03 F14 P13 V02",
    "E12 P14 Q10 Y04",
    "Y13 E03 Y14 E04",
    "S04 S03 E14 S14",
    "V04 E13 S13 Q02",
    "I10 I02 V14 V03",
    "P00 Q04 Z04 S01",
    "I04 Q14 I14 Z14",
    "V13 Q03 I03 S12",
    "Y00 Z03 V01 E11",
    "Q13 Z13 V12 I13",
    "S11 E00 S00 Z02",
    "Q01 R10 I01 Q12",
    "Z12 V11 I12 V00",
    "Z01 Q11 I11 R14",
    "X Z11 Q00 R13",
    "I00 R04 R03 R12",
    "R02 R01 Z00 Z10",
    "R00 R11",
)
BF = jnp.bfloat16
F32 = jnp.float32
MESH = pl.DeviceIdType.MESH


def nn(a, b):
    return jnp.dot(a, b, preferred_element_type=F32)


def nt(a, b):
    return lax.dot_general(a, b, (((1,), (1,)), ((), ())), preferred_element_type=F32)


def tn(a, b):
    return lax.dot_general(a, b, (((0,), (0,)), ((), ())), preferred_element_type=F32)


def kernel(
    tok, gw, uw, dw, gm, um, dm, og,
    mixed_o, ig_o, gg_o, ug_o, dg_o,
    ta, gb, to, go, gwo, uwo, dwo, wgu, kd, keep,
    pf, pp, ph, pr, hd, ho, mp, mz, mr, mr0, p2, ir, si, iz, sm, mx, gwv, uwv, dwv, gv,
    s_ax, s_bz, s_w, s_bx, s_bh, s_az, s_rh, s_ry, s_ay, s_av, s_ho, s_to, s_mz, s_mzh, s_ix, s_iz, s_mx,
    r_ax, r_bz, r_w, r_bx, r_az, r_rh, r_ry, r_ay, r_av, r_ho, r_to, r_mz, r_ix, r_iz, r_mx,
    l_w, l_o,
):
    row, col = lax.axis_index("row"), lax.axis_index("col")
    z, x = row // NX, row % NX
    y, k = col // 2, col % 2

    def dev(dz, dx, dy, core):
        r = ((z + dz + NZ) % NZ) * NX + (x + dx) % NX
        return (r, ((y + dy) % NY) * 2 + core)

    sib = dev(0, 0, 0, 1 - k)

    def send(src, dst, ss, rs, to_dev):
        pltpu.make_async_remote_copy(
            src_ref=src, dst_ref=dst, send_sem=ss, recv_sem=rs, device_id=to_dev, device_id_type=MESH
        ).start()

    def local(src, dst, sem):
        pltpu.make_async_copy(src, dst, sem).start()

    def wait(ref, sem):
        pltpu.make_async_copy(ref, ref, sem).wait()

    def rows(start, size):
        return pl.ds(pl.multiple_of(start, 16), size)

    local(gw, gwv, l_w.at[0])
    local(uw, uwv, l_w.at[1])
    local(dw, dwv, l_w.at[2])

    bar = pltpu.get_barrier_semaphore()
    partners = [sib]
    partners += [dev(0, e, 0, c) for e in range(1, NX) for c in (0, 1)]
    partners += [dev(e, 0, 0, c) for e in range(1, NZ) for c in (0, 1)]
    partners += [dev(0, 0, e, k) for e in range(1, NY)]
    for p in partners:
        pl.semaphore_signal(bar, inc=1, device_id=p, device_id_type=MESH)
    pl.semaphore_wait(bar, len(partners))

    def part_of(core, c):
        return rows(core * H + c * T, T)

    def block(c, s):
        return rows((c * NZ + s) * S + x * T, T)

    def start_tokens(c):
        mine = block(c, 0)
        for e in (1, 3, 2):
            for core in (0, 1):
                send(tok.at[part_of(core, c)], ta.at[k, mine], s_ax, r_ax.at[c], dev(0, e, 0, core))
        send(tok.at[part_of(1 - k, c)], ta.at[k, mine], s_ax, r_ax.at[c], sib)
        local(tok.at[part_of(k, c)], ta.at[k, mine], r_ax.at[c])

    def start_grads(c):
        send(og.at[part_of(1 - k, c)], gb.at[k, block(c, 0)], s_bz, r_bz.at[c, 0], sib)
        local(og.at[part_of(k, c)], gb.at[k, block(c, 0)], r_bz.at[c, 0])
        for e in (1, -1):
            t = SLOT[-e % NZ]
            for core in (0, 1):
                send(og.at[part_of(core, c)], gb.at[k, block(c, t)], s_bz, r_bz.at[c, t], dev(e, 0, 0, core))

    def forward_tokens(c, s):
        d = DZ[s]
        r = pl.ds((c * NZ + s) * S, S)
        if s == 0:
            wait(ta.at[:, r], r_ax.at[c])
        for j in (0, 1):
            if s:
                wait(ta.at[j, r], r_az.at[c, s, j])
            ahead = (1, -1) if s == 0 else (-1 if d > 0 else 1,)
            if s == 7 or (abs(d) == 3 and (d < 0) != (j == 1)):
                ahead = ()
            for e in ahead:
                t = SLOT[(d - e) % NZ]
                send(ta.at[j, r], ta.at[j, pl.ds((c * NZ + t) * S, S)], s_az.at[j], r_az.at[c, t, j], dev(e, 0, 0, k))

    def forward_grads(c, s):
        d = DZ[s]
        mine = block(c, s)
        wait(gb.at[:, pl.ds(0, T)], r_bz.at[c, s])
        e = -1 if d > 0 else 1
        if 0 < abs(d) < 4:
            t = SLOT[(d - e) % NZ]
            there = block(c, t)
            if abs(d) < 3:
                send(gb.at[:, mine], gb.at[:, there], s_bh.at[0], r_bz.at[c, t], dev(e, 0, 0, k))
            else:
                j = 0 if d < 0 else 1
                send(gb.at[j, mine], gb.at[j, there], s_bh.at[1], r_bz.at[c, t], dev(e, 0, 0, k))
        for e in (1, 3, 2):
            send(gb.at[:, mine], gb.at[:, mine], s_bx.at[e - 1], r_bx.at[c, s], dev(0, e, 0, k))

    def start_weights():
        send(gw, gwo, s_w.at[0], r_w.at[0], sib)
        send(uw, uwo, s_w.at[1], r_w.at[1], sib)
        send(dw, dwo, s_w.at[2], r_w.at[2], sib)

    def masks():
        unit = (row * U + lax.broadcasted_iota(jnp.int32, (U, 112), 0)) // BLOCK
        left = (unit == lax.broadcasted_iota(jnp.int32, (U, 112), 1)).astype(F32)
        feat = (y * F + lax.broadcasted_iota(jnp.int32, (32, F), 1)) // BLOCK
        right = (feat == lax.broadcasted_iota(jnp.int32, (32, F), 0)).astype(F32)
        for i, ref in enumerate((gm, um, dm)):
            keep[i] = nn(nt(left, ref[...].astype(F32)), right).astype(BF)

    def keep_weights(core, g_ref, u_ref, d_ref):
        c = pl.ds(pl.multiple_of(core * FC, FC), FC)
        wgu[0:U, c] = keep[0, :, c] * g_ref[...]
        wgu[U : 2 * U, c] = keep[1, :, c] * u_ref[...]
        kd[0:U, c] = keep[2, :, c] * d_ref[...]
        kd[U:UP, c] = jnp.zeros((UP - U, FC), BF)

    halves = (slice(0, CUT), slice(CUT, W))

    def stage1(c, slots):
        r = pl.ds((c * NZ + slots[0]) * S, len(slots) * S)
        for s in slots:
            wait(gb.at[:, pl.ds(0, 3 * T)], r_bx.at[c, s])
        both = nt(ta[0, r, :], wgu[:, 0:FC]) + nt(ta[1, r, :], wgu[:, FC:F])
        back = nt(gb[0, r, :], kd[:, 0:FC]) + nt(gb[1, r, :], kd[:, FC:F])
        pf[r, 0 : 2 * U] = both
        pf[r, 2 * U : W] = back
        pp[r, 0 : 2 * U] = both.astype(BF)
        pp[r, 2 * U : W] = back.astype(BF)
        for s in slots:
            g = c * NZ + s
            far = rows(g * S + (y + 2) % NY * T, T)
            for way, cols in enumerate(halves):
                send(pp.at[far, cols], ph.at[pl.ds(g * T, T), cols], s_rh.at[way], r_rh.at[c, s], dev(0, 0, 1 - 2 * way, k))

    def pass_sums(c, s):
        g = c * NZ + s
        r = pl.ds(g * T, T)
        wait(pp.at[pl.ds(0, T)], r_rh.at[c, s])
        for way, cols in enumerate(halves):
            there = rows(g * S + (y + 1 + 2 * way) % NY * T, T)
            pp[there, cols] = (pf[there, cols] + ph[r, cols].astype(F32)).astype(BF)
            send(pp.at[there], pr.at[way, r], s_ry.at[way], r_ry.at[c, s], dev(0, 0, 1 - 2 * way, k))

    def elementwise(c, s):
        g = c * NZ + s
        wait(pp.at[pl.ds(0, 2 * T)], r_ry.at[c, s])
        mine = rows(g * S + y * T, T)
        r = pl.ds(g * T, T)
        tot = pf[mine, :] + (pr[0, r, :].astype(F32) + pr[1, r, :].astype(F32))
        gate, up, hg = tot[:, 0:U], tot[:, U : 2 * U], tot[:, 2 * U : 3 * U]
        sig = 1.0 / (1.0 + jnp.exp(-gate))
        act = gate * sig
        dgate = hg * up * sig * (1.0 + gate * (1.0 - sig))
        dup = hg * act
        hd[mine, :] = jnp.concatenate([dgate, dup, act * up, jnp.zeros((T, UP - U), F32)], axis=1).astype(BF)

    def share(c, s):
        g = c * NZ + s
        mine = rows(g * S + y * T, T)
        for way in (0, 1):
            send(hd.at[mine], hd.at[mine], s_ay.at[way], r_ay.at[c, s, way], dev(0, 0, 1 - 2 * way, k))

    def share_on(c, s):
        g = c * NZ + s
        for way, cols in enumerate(halves):
            there = rows(g * S + (y + 3 - 2 * way) % NY * T, T)
            wait(hd.at[there], r_ay.at[c, s, way])
            send(hd.at[there, cols], hd.at[there, cols], s_av.at[way], r_av.at[c, s], dev(0, 0, 1 - 2 * way, k))

    def stage2(c, slots):
        r = pl.ds((c * NZ + slots[0]) * S, len(slots) * S)
        for s in slots:
            wait(hd.at[pl.ds(0, T)], r_av.at[c, s])
        mp[r, :] = nn(hd[r, 2 * U : W], kd[...])
        p2[r, :] = nn(hd[r, 0 : 2 * U], wgu[...]).astype(BF)
        send(hd.at[r], ho.at[r], s_ho, r_ho, sib)

    def send_inputs(c, s):
        g = c * NZ + s
        for e in (1, 3, 2):
            other = (x + e) % NX
            send(p2.at[rows(g * S + other * T, T)], ir.at[e - 1, pl.ds(g * T, T)], s_ix.at[e - 1], r_ix.at[c, s], dev(0, e, 0, k))

    def pass_mixed(c, s):
        d = DZ[s]
        r = pl.ds((c * NZ + s) * S, S)
        way = 0 if d < 0 else 1
        ahead = dev(-1 if d < 0 else 1, 0, 0, k)
        if s == 7:
            mz[r, :] = mp[r, :].astype(BF)
            for way, t in ((0, 6), (1, 5)):
                half = slice(way * FC, (way + 1) * FC)
                there = pl.ds((c * NZ + t) * S, S)
                send(mz.at[r, half], mr.at[there, half], s_mzh.at[way], r_mz.at[c, t], dev(2 * way - 1, 0, 0, k))
        elif s:
            if abs(d) == 3:
                half = slice(way * FC, (way + 1) * FC)
                rest = slice((1 - way) * FC, (2 - way) * FC)
                mz[r, rest] = mp[r, rest].astype(BF)
                wait(mr.at[r, half], r_mz.at[c, s])
                mz[r, half] = (mp[r, half] + mr[r, half].astype(F32)).astype(BF)
            else:
                wait(mr.at[r], r_mz.at[c, s])
                mz[r, :] = (mp[r, :] + mr[r, :].astype(F32)).astype(BF)
            if abs(d) == 1:
                send(mz.at[r], mr0.at[c, way], s_mz.at[way], r_mz.at[c, 7 * way], ahead)
            else:
                t = s - 2
                send(mz.at[r], mr.at[pl.ds((c * NZ + t) * S, S)], s_mz.at[way], r_mz.at[c, t], ahead)
        else:
            wait(mr0.at[c, 0], r_mz.at[c, 0])
            wait(mr0.at[c, 1], r_mz.at[c, 7])
            tot = mp[r, :] + (mr0[c, 0].astype(F32) + mr0[c, 1].astype(F32))
            sm[c, 0] = tot[:, 0:FC]
            sm[c, 1] = tot[:, FC:F]
            mine = rows(x * T, T)
            for e in (1, 3, 2):
                other = rows((x + e) % NX * T, T)
                for core in (0, 1):
                    send(sm.at[c, core, other], mx.at[c, k, mine], s_mx, r_mx.at[c], dev(0, e, 0, core))
            send(sm.at[c, 1 - k, mine], mx.at[c, k, mine], s_mx, r_mx.at[c], sib)
            local(sm.at[c, k, mine], mx.at[c, k, mine], r_mx.at[c])

    def reduce_inputs(c, s):
        d = DZ[s]
        g = c * NZ + s
        wait(p2.at[pl.ds(0, 3 * T)], r_ix.at[c, s])
        r = pl.ds(g * T, T)
        own = p2[rows(g * S + x * T, T), :].astype(F32)
        tot = ((own + ir[0, r, :].astype(F32)) + (ir[1, r, :].astype(F32) + ir[2, r, :].astype(F32))).astype(BF)
        si[0, r, :] = tot[:, 0:FC]
        si[1, r, :] = tot[:, FC:F]
        t = pl.ds((c * NZ + SLOT[-d % NZ]) * T, T)
        if s:
            for core in (0, 1):
                send(si.at[core, r], iz.at[k, t], s_iz, r_iz.at[c], dev(d, 0, 0, core))
        else:
            send(si.at[1 - k, r], iz.at[k, t], s_iz, r_iz.at[c], sib)
            local(si.at[k, r], iz.at[k, t], r_iz.at[c])

    def each(step, c, g):
        for s in GROUPS[g]:
            step(c, s)

    def finish_weights():
        wait(gwo, r_w.at[0])
        wait(uwo, r_w.at[1])
        wait(dwo, r_w.at[2])
        keep_weights(1 - k, gwo, uwo, dwo)

    def swap_inputs():
        send(ta.at[1 - k], to, s_to.at[0], r_to.at[0], sib)
        send(gb.at[1 - k], go, s_to.at[1], r_to.at[1], sib)

    def begin():
        masks()
        wait(gwv, l_w.at[0])
        wait(uwv, l_w.at[1])
        wait(dwv, l_w.at[2])
        keep_weights(k, gwv, uwv, dwv)

    steps = {
        "A": start_tokens,
        "G": start_grads,
        "F": lambda c, g: each(forward_tokens, c, g),
        "B": lambda c, g: each(forward_grads, c, g),
        "P": lambda c, g: stage1(c, GROUPS[g]),
        "Y": lambda c, g: each(pass_sums, c, g),
        "V": lambda c, g: each(share_on, c, g),
        "E": lambda c, g: each(elementwise, c, g),
        "S": lambda c, g: each(share, c, g),
        "Q": lambda c, g: stage2(c, GROUPS[g]),
        "I": lambda c, g: each(send_inputs, c, g),
        "Z": lambda c, g: each(pass_mixed, c, g),
        "R": lambda c, g: each(reduce_inputs, c, g),
        "W": start_weights,
        "M": begin,
        "N": finish_weights,
        "X": swap_inputs,
    }
    for line in ORDER:
        for step in line.split():
            steps[step[0]](*map(int, step[1:]))

    wait(to, r_to.at[0])
    wait(go, r_to.at[1])
    wait(ho, r_ho)
    own = pl.ds(pl.multiple_of(k * FC, FC), FC)
    for i, out in enumerate((gg_o, ug_o)):
        c = slice(i * U, (i + 1) * U)
        gv[i] = (tn(hd[:, c], ta[k]) + tn(ho[:, c], to[...])) * keep[i, :, own].astype(F32)
        local(gv.at[i], out, l_o.at[i])
    c = slice(2 * U, 3 * U)
    gv[2] = (tn(hd[:, c], gb[k]) + tn(ho[:, c], go[...])) * keep[2, :, own].astype(F32)
    local(gv.at[2], dg_o, l_o.at[2])

    for c in range(NC):
        wait(mx.at[c], r_mx.at[c])
        for core in (0, 1):
            part = [mx[c, core, i * T : (i + 1) * T, :] for i in range(NX)]
            there = slice(core * H + c * T, core * H + (c + 1) * T)
            mixed_o[there, :] = ((part[0] + part[1]) + (part[2] + part[3])).astype(BF)
    for c in range(NC):
        wait(iz.at[:, pl.ds(c * NZ * T, NZ * T)], r_iz.at[c])
        for core in (0, 1):
            part = [iz[core, (c * NZ + i) * T : (c * NZ + i + 1) * T, :].astype(F32) for i in range(NZ)]
            low = (part[0] + part[1]) + (part[2] + part[3])
            high = (part[4] + part[5]) + (part[6] + part[7])
            there = slice(core * H + c * T, core * H + (c + 1) * T)
            ig_o[there, :] = (low + high).astype(BF)

    for i in range(3):
        wait(gv.at[i], l_o.at[i])
    wait(ta.at[0, pl.ds(0, 7 * NC * T)], s_ax)
    wait(ta.at[0, pl.ds(0, 5 * NC * T)], s_bz)
    wait(gb.at[:, pl.ds(0, 4 * NC * T)], s_bh.at[0])
    wait(gb.at[0, pl.ds(0, 2 * NC * T)], s_bh.at[1])
    for i in range(3):
        wait((gwo, uwo, dwo)[i], s_w.at[i])
        wait(gb.at[:, pl.ds(0, NS * T)], s_bx.at[i])
        wait(p2.at[pl.ds(0, NS * T)], s_ix.at[i])
    for j in (0, 1):
        wait(ta.at[j, pl.ds(0, 7 * NC * S)], s_az.at[j])
        wait(pp.at[pl.ds(0, NS * T)], s_ry.at[j])
        wait(hd.at[pl.ds(0, NS * T)], s_ay.at[j])
        wait(pp.at[pl.ds(0, NS * T), halves[j]], s_rh.at[j])
        wait(hd.at[pl.ds(0, NS * T), halves[j]], s_av.at[j])
        wait(to, s_to.at[j])
        wait(mz.at[pl.ds(0, 3 * NC * S)], s_mz.at[j])
        wait(mz.at[pl.ds(0, NC * S), 0:FC], s_mzh.at[j])
    wait(ho, s_ho)
    wait(gb.at[0, pl.ds(0, 15 * NC * T)], s_iz)
    wait(ta.at[:, pl.ds(0, 7 * NC * T)], s_mx)


def per_device(tokens, gate_weight, up_weight, down_weight, gate_mask, up_mask, down_mask, out_grad):
    vmem = pl.BlockSpec(memory_space=pltpu.VMEM)
    hbm = pl.BlockSpec(memory_space=pl.ANY)
    dma = pltpu.SemaphoreType.DMA
    v = pltpu.VMEM
    mixed, input_grad, gate_grad, up_grad, down_grad = pl.pallas_call(
        kernel,
        out_shape=(
            jax.ShapeDtypeStruct((2 * H, FC), BF),
            jax.ShapeDtypeStruct((2 * H, FC), BF),
            jax.ShapeDtypeStruct((U, FC), F32),
            jax.ShapeDtypeStruct((U, FC), F32),
            jax.ShapeDtypeStruct((U, FC), F32),
        ),
        in_specs=[vmem, hbm, hbm, hbm, vmem, vmem, vmem, vmem],
        out_specs=(vmem, vmem, hbm, hbm, hbm),
        scratch_shapes=[
            v((2, NS * S, FC), BF),
            v((2, NS * S, FC), BF),
            v((NS * S, FC), BF),
            v((NS * S, FC), BF),
            v((U, FC), BF),
            v((U, FC), BF),
            v((U, FC), BF),
            v((2 * U, F), BF),
            v((UP, F), BF),
            v((3, U, F), BF),
            v((NS * S, W), F32),
            v((NS * S, W), BF),
            v((NS * T, W), BF),
            v((2, NS * T, W), BF),
            v((NS * S, W), BF),
            v((NS * S, W), BF),
            v((NS * S, F), F32),
            v((NS * S, F), BF),
            v((NS * S, F), BF),
            v((NC, 2, S, F), BF),
            v((NS * S, F), BF),
            v((3, NS * T, F), BF),
            v((2, NS * T, FC), BF),
            v((2, NS * T, FC), BF),
            v((NC, 2, S, FC), F32),
            v((NC, 2, S, FC), F32),
            v((U, FC), BF),
            v((U, FC), BF),
            v((U, FC), BF),
            v((3, U, FC), F32),
            dma, dma, dma((3,)), dma((3,)), dma((2,)), dma((2,)), dma((2,)), dma((2,)), dma((2,)), dma((2,)), dma, dma((2,)), dma((2,)), dma((2,)), dma((3,)), dma, dma,
            dma((NC,)), dma((NC, 8)), dma((3,)), dma((NC, 8)), dma((NC, 8, 2)), dma((NC, 8)), dma((NC, 8)), dma((NC, 8, 2)), dma((NC, 8)), dma, dma((2,)), dma((NC, 8)), dma((NC, 8)), dma((NC,)), dma((NC,)),
            dma((3,)), dma((3,)),
        ],
        compiler_params=pltpu.CompilerParams(
            collective_id=0, has_side_effects=True, vmem_limit_bytes=60 << 20
        ),
        cost_estimate=pl.CostEstimate(flops=9_000_000_000, bytes_accessed=8 << 20, transcendentals=120_000),
        name="sublayer",
    )(tokens, gate_weight.T, up_weight.T, down_weight, gate_mask, up_mask, down_mask.T, out_grad)
    return mixed, input_grad, gate_grad.T, up_grad.T, down_grad


def solution(mesh):
    return jax.shard_map(
        per_device,
        mesh=mesh,
        in_specs=(
            P("row", "col"), P("col", "row"), P("col", "row"), P("row", "col"), P(), P(), P(), P("row", "col"),
        ),
        out_specs=(P("row", "col"), P("row", "col"), P("col", "row"), P("col", "row"), P("row", "col")),
        check_vma=False,
    )
```
